128 devices in a mesh: rows: 32 (over z, y, core), cols: 4 (over x).
Axes of the slice: x: 4, y: 4, z: 4, core: 2. Of those that a mesh axis runs over, the one named last changes fastest.
Arguments:
- rhs: float32 [131072, 128], P('rows'), may hold values from -6 to 6
- guess: float32 [131072, 128], P('rows'), may hold values from -3 to 3
- near: bfloat16 [2, 512, 16, 256, 256], P(None, 'rows', 'cols'), may hold values from -0.09375 to 0.09375
- near_cols: int32 [512, 16], P('rows', 'cols'), may hold values from 0 to 511, as said below
- far_u: bfloat16 [2, 512, 32, 32, 256], P(None, 'rows', 'cols'), may hold values from -0.1875 to 0.1875
- far_cols: int32 [512, 32], P('rows', 'cols'), may hold values from 0 to 511, as said below
- far_count: int32 [512], P('rows'), may hold values from 1 to 32, as said below
- basis: bfloat16 [2, 512, 32, 256], P(None, 'rows'), may hold values from -0.375 to 0.375
Outputs:
- solution: float32 [131072, 128], P('rows')
The draws below stay inside these ranges and needn't reach their ends.
Inputs may be any that keep to these rules, and one draw needn't show every extreme that they name: `near_cols`: the near blocks of block row i lie within 8 blocks of block i, block i among them. `far_cols`: A far block of block row i lies more than 8 blocks from block i, counted around the end. Only the first far_count[i] slots of block row i are used.
All inputs are finite; a program needn't handle non-finite values.
Results may differ from the reference program's by a relative error of at most 0.0025.
Values may be sent and summed in bfloat16 or wider, within the bound.
No kernel may reach another device: no remote copies, remote signals or barrier semaphores. Data moves between devices by JAX's collectives and lax.ppermute only.
A program may use at most 128 MiB of HBM per device.

```python
import jax
import jax.numpy as jnp
from jax import lax

B = 256
K = 32
R = 64
NEAR = 16
FAR = 32
HALF = 8
BLK_DEV = 16
NB = 512
N = 131072


def draw_near_cols(key, part):
    key = jax.random.fold_in(key, 11)
    key_pick, key_order = jax.random.split(key)
    candidates = jnp.concatenate([jnp.arange(-HALF + 1, 0), jnp.arange(1, HALF)]).astype(jnp.int32)
    scores = jax.random.randint(key_pick, (NB, 2 * HALF - 2), 0, 2 ** 30)
    picked = jnp.argsort(scores, axis=1)[:, :NEAR - 3]
    offsets = candidates[picked]
    fixed = jnp.broadcast_to(jnp.array([0, HALF, -HALF], jnp.int32), (NB, 3))
    offsets = jnp.concatenate([fixed, offsets], axis=1)
    order = jnp.argsort(jax.random.randint(key_order, (NB, NEAR), 0, 2 ** 30), axis=1)
    offsets = jnp.take_along_axis(offsets, order, axis=1)
    rows_here = jnp.arange(NB, dtype=jnp.int32)[:, None]
    return jnp.clip(rows_here + offsets, 0, NB - 1).astype(jnp.int32)


def draw_far_cols(key, part):
    key = jax.random.fold_in(key, 12)
    spread = jax.random.randint(key, (NB, FAR), 0, NB - 2 * HALF - 1)
    rows_here = jnp.arange(NB, dtype=jnp.int32)[:, None]
    slots = jnp.arange(FAR, dtype=jnp.int32)[None, :]
    spread = jnp.where((rows_here == NB - HALF - 1) & (slots == 0), 0, spread)
    spread = jnp.where((rows_here == HALF) & (slots == 0), NB - 2 * HALF - 2, spread)
    return ((rows_here + HALF + 1 + spread) % NB).astype(jnp.int32)


def draw_far_count(key, part):
    key = jax.random.fold_in(key, 13)
    key_count, key_full = jax.random.split(key)
    counts = jax.random.randint(key_count, (NB,), 1, FAR + 1)
    groups = NB // BLK_DEV
    chosen = jnp.arange(groups, dtype=jnp.int32) * BLK_DEV + jax.random.randint(key_full, (groups,), 0, BLK_DEV)
    full = jnp.any(jnp.arange(NB, dtype=jnp.int32)[:, None] == chosen[None, :], axis=1)
    return jnp.where(full, FAR, counts).astype(jnp.int32)


def level_of(stream_key, dims, shards, low, high):
    gain = 1.0
    for position, blocks in shards:
        steps = jax.random.uniform(jax.random.fold_in(jax.random.fold_in(stream_key, 6), position), (blocks,), jnp.float32, low / len(shards), high / len(shards))
        gain = gain * jnp.repeat(jnp.exp(steps), dims[position] // blocks).reshape((-1,) + (1,) * (len(dims) - 1 - position))
    return gain


def normal_values(key, extent, scale, reach, shards=(), held_as=jnp.bfloat16):
    entries = scale * jax.random.normal(key, extent, jnp.float32)
    if shards:
        entries = entries * level_of(key, extent, shards, -0.22, 0.18)
    return jnp.clip(entries, -reach, reach).astype(held_as)


def setup_inputs(seed: int = 0) -> dict:
    key_list = jax.random.split(jax.random.key(seed), 9)
    return {
        "rhs": normal_values(key_list[0], (N, 2 * R), 1.0, 6.0, ((0, 32),), jnp.float32),
        "guess": normal_values(key_list[1], (N, 2 * R), 0.5, 3.0, ((0, 32),), jnp.float32),
        "near": normal_values(key_list[2], (2, NB, NEAR, B, B), (NEAR * B) ** -0.5, 0.09375, ((1, 32), (2, 4))),
        "near_cols": draw_near_cols(jax.random.fold_in(key_list[8], 71), 0),
        "far_u": normal_values(key_list[4], (2, NB, FAR, K, B), (FAR * K) ** -0.5, 0.1875, ((1, 32), (2, 4))),
        "far_cols": draw_far_cols(jax.random.fold_in(key_list[8], 71), 0),
        "far_count": draw_far_count(jax.random.fold_in(key_list[8], 71), 0),
        "basis": normal_values(key_list[7], (2, NB, K, B), B ** -0.5, 0.375, ((1, 32),)),
    }


def swap_halves(x):
    return jnp.concatenate([-x[..., R:], x[..., :R]], axis=-1)

def inner(a, b):
    return jnp.einsum('nhr,nhs->rs', a.reshape(-1, 2, R), b.reshape(-1, 2, R), precision=lax.Precision.HIGHEST)

def times(a, m):
    return jnp.einsum('nhr,rs->nhs', a.reshape(-1, 2, R), m, precision=lax.Precision.HIGHEST).reshape(a.shape)

def lower_inverse(low):
    return lax.linalg.triangular_solve(low, jnp.eye(low.shape[0], dtype=low.dtype), left_side=True, lower=True)

def matmul(a, b):
    return jnp.dot(a, b, precision=lax.Precision.HIGHEST)

def operate(vec, near, near_cols, far_u, far_cols, far_count, basis):
    vb = vec.astype(jnp.bfloat16)
    blocks = vb.reshape(NB, B, 2 * R)
    jblocks = swap_halves(blocks)
    coef = jnp.einsum('jkb,jbc->jkc', basis[0].astype(jnp.float32), blocks.astype(jnp.float32))
    coef = coef + jnp.einsum('jkb,jbc->jkc', basis[1].astype(jnp.float32), jblocks.astype(jnp.float32))
    coef = coef.astype(jnp.bfloat16)
    jcoef = swap_halves(coef)

    def one_row(items):
        near_re, near_im, ncols, far_re, far_im, fcols, count = items
        near_y = jnp.einsum('sab,sbc->ac', near_re.astype(jnp.float32), blocks[ncols].astype(jnp.float32))
        near_y = near_y + jnp.einsum('sab,sbc->ac', near_im.astype(jnp.float32), jblocks[ncols].astype(jnp.float32))
        used = (jnp.arange(FAR) < count).astype(jnp.float32)[:, None, None]
        far_y = jnp.einsum('skb,skc->bc', far_re.astype(jnp.float32), coef[fcols].astype(jnp.float32) * used)
        far_y = far_y + jnp.einsum('skb,skc->bc', far_im.astype(jnp.float32), jcoef[fcols].astype(jnp.float32) * used)
        return near_y + far_y
    rows_out = lax.map(one_row, (near[0], near[1], near_cols, far_u[0], far_u[1], far_cols, far_count))
    return vec + rows_out.reshape(N, 2 * R)

def reference(rhs, guess, near, near_cols, far_u, far_cols, far_count, basis):

    def apply_op(vec):
        return operate(vec, near, near_cols, far_u, far_cols, far_count, basis)
    first = rhs - apply_op(guess)
    low0 = jnp.linalg.cholesky(inner(first, first))
    upper0 = low0.T
    basis_one = times(first, lower_inverse(low0).T)
    image = apply_op(basis_one)
    h11 = inner(basis_one, image)
    image = image - times(basis_one, h11)
    low1 = jnp.linalg.cholesky(inner(image, image))
    h21 = low1.T
    basis_two = times(image, lower_inverse(low1).T)
    image = apply_op(basis_two)
    h12 = inner(basis_one, image)
    h22 = inner(basis_two, image)
    image = image - times(basis_one, h12) - times(basis_two, h22)
    h32 = jnp.linalg.cholesky(inner(image, image)).T
    zeros = jnp.zeros((R, R), jnp.float32)
    hbar = jnp.concatenate([jnp.concatenate([h11, h12], 1), jnp.concatenate([h21, h22], 1), jnp.concatenate([zeros, h32], 1)], 0)
    normal = matmul(hbar.T, hbar)
    target = jnp.concatenate([matmul(h11.T, upper0), matmul(h12.T, upper0)], 0)
    inverse_low = lower_inverse(jnp.linalg.cholesky(normal))
    weights = matmul(inverse_low.T, matmul(inverse_low, target))
    return guess + times(basis_one, weights[:R]) + times(basis_two, weights[R:])
```

```python
import functools

import jax
import jax.numpy as jnp
from jax import lax
from jax.experimental import pallas as pl
from jax.experimental.pallas import tpu as pltpu
from jax.sharding import PartitionSpec as P

B = 256
K = 32
R = 64
HALF = 8
SIDE = 4
CORES = 2
NBLK = 16
BF = jnp.bfloat16
F32 = jnp.float32


def row_id(z, y, k):
    return (z * SIDE + y) * CORES + k


def shift_y(d):
    return [
        (row_id(z, y, k), row_id(z, (y + d) % SIDE, k))
        for z in range(SIDE) for y in range(SIDE) for k in range(CORES)
    ]


def shift_z(d):
    return [
        (row_id(z, y, k), row_id((z + d) % SIDE, y, k))
        for z in range(SIDE) for y in range(SIDE) for k in range(CORES)
    ]


def send_x(a, d):
    return lax.ppermute(a, "cols", [(x, (x + d) % SIDE) for x in range(SIDE)])


def send_y(a, d):
    return lax.ppermute(a, "rows", shift_y(d))


def send_z(a, d):
    return lax.ppermute(a, "rows", shift_z(d))


def send_core(a):
    return lax.ppermute(a, "rows", [(r, r ^ 1) for r in range(SIDE * SIDE * CORES)])


def send_row(a, d):
    n = SIDE * SIDE * CORES
    return lax.ppermute(a, "rows", [(r, (r + d) % n) for r in range(n)])


def swap_halves(x):
    return jnp.concatenate([-x[..., R:], x[..., :R]], axis=-1)


def dot(a, b):
    return lax.dot_general(a, b, (((1,), (0,)), ((), ())), preferred_element_type=F32)


def dot_t(a, b):
    return lax.dot_general(a, b, (((0,), (0,)), ((), ())), preferred_element_type=F32)


ORDER, NCOL, FPOS, USED, VSLOT = 0, 16, 80, 208, 224


def matvec_kernel(n_v, coef, tab, *refs):
    near, far, basis = refs[:3]
    pieces = refs[3 : 3 + n_v]
    cpieces = refs[3 + n_v : 3 + n_v + 16]
    rest = refs[3 + n_v + 16 :]
    p0, p1, p2, p3, own = rest[:5]
    cpart = rest[5] if coef else None
    vj, cs, fx, vsem, csem = rest[5 + coef :]
    t = pl.program_id(0)
    row = tab[ORDER + t]

    @pl.when(t == 0)
    def _():
        copies = []
        n = 0
        for piece in pieces:
            for b in range(piece.shape[0]):
                slot = tab[VSLOT + n]
                copies.append(
                    pltpu.make_async_copy(piece.at[b], vj.at[slot, pl.ds(0, B), :], vsem.at[n])
                )
                n += 1
        for m, piece in enumerate(cpieces):
            copies.append(pltpu.make_async_copy(piece, cs.at[pl.ds(32 * m, 32)], csem.at[m]))
        for c in copies:
            c.start()
        for c in copies:
            c.wait()

        def body(b, carry):
            x = vj[b, pl.ds(0, B), :]
            vj[b, pl.ds(B, B), :] = swap_halves(x)
            return carry

        lax.fori_loop(0, 32, body, 0)
        for b in range(NBLK):
            own[b] = vj[HALF + b, pl.ds(0, B), :]

    acc = jnp.zeros((B, 2 * R), F32)
    for s in range(4):
        c = tab[NCOL + row * 4 + s]
        acc = acc + dot(near[0, 0, s], vj[c, pl.ds(0, B), :])
        acc = acc + dot(near[1, 0, s], vj[c, pl.ds(B, B), :])
    used = tab[USED + row]
    for s in range(8):
        pos = tab[FPOS + row * 8 + s]
        fx[pl.ds(s * K, K), :] = jnp.where(s < used, cs[pos], jnp.zeros((K, 2 * R), BF))
    x = fx[...]
    acc = acc + dot_t(far[0, 0].reshape(B, B), x)
    acc = acc + dot_t(far[1, 0].reshape(B, B), swap_halves(x))
    pb = acc.astype(BF)
    q = lax.rem(t, 4)
    phase = t // 4
    for k, ref in enumerate((p2, p1, p3)):
        @pl.when(phase == k)
        def _(ref=ref):
            ref[q] = pb

    @pl.when(phase == 3)
    def _():
        p0[q] = acc

    if coef:
        cpart[row] = (dot(basis[0, 0], pb) + dot(basis[1, 0], swap_halves(pb))).astype(BF)


def matvec(tab, near, far, basis, pieces, cpieces, coef):
    anyspec = pl.BlockSpec(memory_space=pl.ANY)
    full = lambda shape: pl.BlockSpec(shape, lambda t, tab: (0,) * len(shape))
    quarter = (4, B, 2 * R)
    outs = [jax.ShapeDtypeStruct(quarter, F32)] + [jax.ShapeDtypeStruct(quarter, BF)] * 3
    outs.append(jax.ShapeDtypeStruct((NBLK, B, 2 * R), BF))
    out_specs = [full(quarter)] * 4 + [full((NBLK, B, 2 * R))]
    if coef:
        outs.append(jax.ShapeDtypeStruct((NBLK, K, 2 * R), BF))
        out_specs.append(full((NBLK, K, 2 * R)))
    grid_spec = pltpu.PrefetchScalarGridSpec(
        num_scalar_prefetch=1,
        grid=(NBLK,),
        in_specs=[
            pl.BlockSpec((2, 1, 4, B, B), lambda t, tab: (0, tab[ORDER + t], 0, 0, 0)),
            pl.BlockSpec((2, 1, 8, K, B), lambda t, tab: (0, tab[ORDER + t], 0, 0, 0)),
            pl.BlockSpec((2, 1, K, B), lambda t, tab: (0, tab[ORDER + t], 0, 0)),
        ] + [anyspec] * (len(pieces) + 16),
        out_specs=out_specs,
        scratch_shapes=[
            pltpu.VMEM((32, 2 * B, 2 * R), BF),
            pltpu.VMEM((512, K, 2 * R), BF),
            pltpu.VMEM((B, 2 * R), BF),
            pltpu.SemaphoreType.DMA((32,)),
            pltpu.SemaphoreType.DMA((16,)),
        ],
    )
    return pl.pallas_call(
        functools.partial(matvec_kernel, len(pieces), coef),
        out_shape=outs,
        grid_spec=grid_spec,
        compiler_params=pltpu.CompilerParams(
            dimension_semantics=("arbitrary",), vmem_limit_bytes=40 * 2 ** 20
        ),
        cost_estimate=pl.CostEstimate(
            flops=2_700_000_000, bytes_accessed=28_000_000, transcendentals=0
        ),
    )(tab, near, far, basis, *pieces, *cpieces)


def gather_coef(c):
    a, b = c[:8], c[8:]
    a_all = jnp.concatenate([a] + [send_y(a, d) for d in (1, 2, 3)], axis=0)
    b_all = jnp.concatenate([b] + [send_z(b, d) for d in (1, 2, 3)], axis=0)
    mine = [a_all] + [send_z(a_all, d) for d in (1, 2, 3)]
    mine += [b_all] + [send_y(b_all, d) for d in (1, 2, 3)]
    return mine + [send_core(m) for m in mine]


def gather_vector(v):
    low, high = v[:2], v[2:]
    lows = [low] + [send_x(low, d) for d in (1, 2, 3)]
    highs = [high] + [send_x(high, d) for d in (1, 2, 3)]
    from_prev = [send_row(h, 1) for h in highs]
    from_next = [send_row(l, -1) for l in lows]
    return lows + highs + from_prev + from_next


def sum_x(own, parts):
    return (own + parts[1]) + (parts[0] + parts[2])


def all_sum(m):
    m = m + send_core(m)
    for send in (send_x, send_y, send_z):
        m = sum_x(m, [send(m, d) for d in (1, 2, 3)])
    return m


def inner(a, b):
    full = lax.dot_general(
        a.reshape(-1, 2 * R), b.reshape(-1, b.shape[-1]), (((0,), (0,)), ((), ())),
        precision=lax.Precision.HIGHEST, preferred_element_type=F32,
    )
    n = b.shape[-1] // (2 * R)
    full = full.reshape(2, R, n, 2, R)
    return (full[0, :, :, 0] + full[1, :, :, 1]).reshape(R, n * R)


def lower_inverse(low):
    return lax.linalg.triangular_solve(
        low, jnp.eye(low.shape[0], dtype=low.dtype), left_side=True, lower=True
    )


def matmul(a, b):
    return jnp.dot(a, b, precision=lax.Precision.HIGHEST)


def coefs(basis, blocks):
    out = jnp.einsum("jkb,jbc->jkc", basis[0], blocks, preferred_element_type=F32)
    return out + jnp.einsum(
        "jkb,jbc->jkc", basis[1], swap_halves(blocks), preferred_element_type=F32
    )


def shards(rhs, guess, near, near_cols, far_u, far_cols, far_count, basis):
    me_r = lax.axis_index("rows")
    me_c = lax.axis_index("cols")
    z, y, k = me_r // 8, (me_r // 2) % SIDE, me_r % 2
    ints = lambda *v: jnp.array(v, jnp.int32)

    lane = jnp.arange(16, dtype=jnp.int32)
    order = (me_c + ints(2, 1, 3, 0)[lane // 4]) % SIDE + 4 * (lane % 4)
    ncol = (near_cols - (me_r * NBLK - HALF)).reshape(-1)
    owner, b = far_cols // NBLK, far_cols % NBLK
    dz, dy = (z - owner // 8) % SIDE, (y - (owner // 2) % SIDE) % SIDE
    other, half = (owner % 2 != k).astype(jnp.int32), b // 8
    inside = jnp.where(half == 0, dz * 4 + dy, dy * 4 + dz)
    fpos = (((other * 2 + half) * 16 + inside) * 8 + b % 8).reshape(-1)
    used = jnp.clip(far_count - me_c * 8, 0, 8)
    e = (me_c - jnp.arange(4, dtype=jnp.int32)) % SIDE
    pair = (e[:, None] + ints(0, 4)).reshape(-1)
    head = [order, ncol, fpos, used]
    slots_first = jnp.concatenate([HALF + lane, lane[:8], HALF + 16 + lane[:8]])
    slots_next = jnp.concatenate([HALF + pair, HALF + 8 + pair, pair, HALF + 16 + pair])
    tab_first = jnp.concatenate(head + [slots_first]).astype(jnp.int32)
    tab_next = jnp.concatenate(head + [slots_next]).astype(jnp.int32)

    gb = guess.astype(BF).reshape(NBLK, B, 2 * R)
    diff = (rhs - guess).reshape(NBLK, B, 2 * R)
    c_guess = coefs(basis, gb)
    cp = gather_coef(c_guess.astype(BF))
    c_diff = coefs(basis, diff.astype(BF))
    pieces = [gb, send_row(gb[8:], 1), send_row(gb[:8], -1)]
    p0, p1, p2, p3, _, cpart = matvec(tab_first, near, far_u, basis, pieces, cp, True)

    def summed(p0, p1, p2, p3):
        parts = [send_x(p, d).astype(F32) for d, p in ((1, p1), (2, p2), (3, p3))]
        return sum_x(p0, parts)

    def summed_coef(cpart):
        parts = [send_x(cpart, d).astype(F32) for d in (1, 2, 3)]
        return sum_x(cpart.astype(F32), parts)

    c_first = c_diff - summed_coef(cpart)
    mine = lax.dynamic_index_in_dim(
        diff.reshape(4, 4, B, 2 * R), me_c, axis=1, keepdims=False
    )
    first = mine - summed(p0, p1, p2, p3)
    cp = gather_coef(c_first.astype(BF))
    pieces = gather_vector(first.astype(BF))
    p0, p1, p2, p3, first_b, cpart = matvec(tab_next, near, far_u, basis, pieces, cp, True)
    c_image = c_first + summed_coef(cpart)
    image = first + summed(p0, p1, p2, p3)
    cp = gather_coef(c_image.astype(BF))
    pieces = gather_vector(image.astype(BF))
    p0, p1, p2, p3, image_b = matvec(tab_next, near, far_u, basis, pieces, cp, False)
    second = image + summed(p0, p1, p2, p3)

    stack = jnp.concatenate([first, image, second], axis=-1)
    gram = jnp.concatenate([inner(image, stack), inner(second, stack)], axis=0)
    gram = all_sum(gram.reshape(-1, 128)).reshape(2 * R, 3 * R)
    normal, target = gram[:, R:], gram[:, :R]
    inverse_low = lower_inverse(jnp.linalg.cholesky(normal))
    weights = matmul(inverse_low.T, matmul(inverse_low, target))

    def times(a, m):
        return jnp.einsum(
            "nhr,rs->nhs", a.astype(F32).reshape(-1, 2, R), m, precision=lax.Precision.HIGHEST
        ).reshape(-1, 2 * R)

    return guess + times(first_b, weights[:R]) + times(image_b, weights[R:])


def solution(mesh):
    in_specs = (
        P("rows", None),
        P("rows", None),
        P(None, "rows", "cols", None, None),
        P("rows", "cols"),
        P(None, "rows", "cols", None, None),
        P("rows", "cols"),
        P("rows"),
        P(None, "rows", None, None),
    )
    return jax.shard_map(
        shards, mesh=mesh, in_specs=in_specs, out_specs=P("rows", None), check_vma=False
    )
```

```python
import functools

import jax
import jax.numpy as jnp
from jax import lax
from jax.experimental import pallas as pl
from jax.experimental.pallas import tpu as pltpu
from jax.sharding import PartitionSpec as P

B = 256
K = 32
R = 64
HALF = 8
SIDE = 4
CORES = 2
NBLK = 16
BF = jnp.bfloat16
F32 = jnp.float32


def row_id(z, y, k):
    return (z * SIDE + y) * CORES + k


def shift_y(d):
    return [
        (row_id(z, y, k), row_id(z, (y + d) % SIDE, k))
        for z in range(SIDE) for y in range(SIDE) for k in range(CORES)
    ]


def shift_z(d):
    return [
        (row_id(z, y, k), row_id((z + d) % SIDE, y, k))
        for z in range(SIDE) for y in range(SIDE) for k in range(CORES)
    ]


def send_x(a, d):
    return lax.ppermute(a, "cols", [(x, (x + d) % SIDE) for x in range(SIDE)])


def send_y(a, d):
    return lax.ppermute(a, "rows", shift_y(d))


def send_z(a, d):
    return lax.ppermute(a, "rows", shift_z(d))


def send_core(a):
    return lax.ppermute(a, "rows", [(r, r ^ 1) for r in range(SIDE * SIDE * CORES)])


def send_row(a, d):
    n = SIDE * SIDE * CORES
    return lax.ppermute(a, "rows", [(r, (r + d) % n) for r in range(n)])


def nn(a, b, precision=None):
    return lax.dot_general(
        a, b, (((1,), (0,)), ((), ())), preferred_element_type=F32, precision=precision
    )


def nt(a, b, precision=None):
    return lax.dot_general(
        a, b, (((1,), (1,)), ((), ())), preferred_element_type=F32, precision=precision
    )


def turn(x):
    return jnp.concatenate([-x[R:], x[:R]], axis=0)


def turn_lanes(x):
    return jnp.concatenate([-x[:, R:], x[:, :R]], axis=1)


def full_spec(shape):
    return pl.BlockSpec(shape, lambda *_: (0,) * len(shape))


ORDER, NCOL, FPOS, USED, VSLOT = 0, 16, 80, 208, 224
QUARTER = (4, 2 * R, B)
VMEM = 56 * 2 ** 20


def coef_of(basis, vec):
    both = nt(basis.reshape(2 * K, B), vec)
    return both[:K] + turn_lanes(both[K:])


def guess_coef_kernel(guess, basis, out):
    for i in range(NBLK):
        g = guess[pl.ds(i * B, B), :].astype(BF)
        both = nn(basis[:, i].reshape(2 * K, B), g)
        out[i] = (both[:K] + turn_lanes(both[K:])).astype(BF)


def guess_coef(guess, basis):
    return pl.pallas_call(
        guess_coef_kernel,
        out_shape=jax.ShapeDtypeStruct((NBLK, K, 2 * R), BF),
        compiler_params=pltpu.CompilerParams(vmem_limit_bytes=VMEM),
    )(guess, basis)


def prepare_kernel(tab, rhs, guess, basis, low, high, mine, cd):
    for i in range(NBLK):
        g = guess[pl.ds(i * B, B), :]
        (low if i < HALF else high)[i % HALF] = g.astype(BF).T
        d = (rhs[pl.ds(i * B, B), :] - g).astype(BF)
        both = nn(basis[:, i].reshape(2 * K, B), d)
        cd[i] = both[:K] + turn_lanes(both[K:])
    for q in range(4):
        at = pl.ds(pl.multiple_of((tab[0] + 4 * q) * B, B), B)
        mine[q] = (rhs[at, :] - guess[at, :]).T


def prepare(tab, rhs, guess, basis):
    vmem = pl.BlockSpec(memory_space=pltpu.VMEM)
    return pl.pallas_call(
        prepare_kernel,
        in_specs=[pl.BlockSpec(memory_space=pltpu.SMEM), vmem, vmem, vmem],
        out_specs=[vmem] * 4,
        out_shape=[
            jax.ShapeDtypeStruct((HALF, 2 * R, B), BF),
            jax.ShapeDtypeStruct((HALF, 2 * R, B), BF),
            jax.ShapeDtypeStruct(QUARTER, F32),
            jax.ShapeDtypeStruct((NBLK, K, 2 * R), F32),
        ],
        compiler_params=pltpu.CompilerParams(vmem_limit_bytes=VMEM),
    )(tab, rhs, guess, basis)


LOOK = 3


def near_kernel(sizes, tab, near, *refs):
    pieces, out = refs[: len(sizes)], refs[len(sizes)]
    vt, nbuf, vsem, nsem = refs[len(sizes) + 1 :]

    def near_copy(t):
        return pltpu.make_async_copy(near.at[:, t], nbuf.at[t], nsem.at[t])

    copies = []
    for piece, size in zip(pieces, sizes):
        for b in range(size):
            n = len(copies)
            copies.append(pltpu.make_async_copy(piece.at[b], vt.at[tab[VSLOT + n]], vsem.at[n]))
    for c in copies:
        c.start()
    for t in range(LOOK):
        near_copy(t).start()
    for c in copies:
        c.wait()

    def body(t, carry):
        @pl.when(t < NBLK - LOOK)
        def _():
            near_copy(t + LOOK).start()

        near_copy(t).wait()
        re = jnp.zeros((2 * R, B), F32)
        im = jnp.zeros((2 * R, B), F32)
        for s in range(4):
            x = vt[tab[NCOL + t * 4 + s]]
            re = re + nt(x, nbuf[t, 0, s])
            im = im + nt(x, nbuf[t, 1, s])
        out[t] = re + turn(im)
        return carry

    lax.fori_loop(0, NBLK, body, 0)


def near_terms(tab, near, pieces):
    anyspec = pl.BlockSpec(memory_space=pl.ANY)
    sizes = [p.shape[0] for p in pieces]
    return pl.pallas_call(
        functools.partial(near_kernel, sizes),
        out_shape=jax.ShapeDtypeStruct((NBLK, 2 * R, B), F32),
        in_specs=[pl.BlockSpec(memory_space=pltpu.SMEM)] + [anyspec] * (1 + len(pieces)),
        out_specs=pl.BlockSpec(memory_space=pltpu.VMEM),
        scratch_shapes=[
            pltpu.VMEM((32, 2 * R, B), BF),
            pltpu.VMEM((NBLK, 2, 4, B, B), BF),
            pltpu.SemaphoreType.DMA((32,)),
            pltpu.SemaphoreType.DMA((NBLK,)),
        ],
        compiler_params=pltpu.CompilerParams(vmem_limit_bytes=VMEM),
        cost_estimate=pl.CostEstimate(
            flops=8_000_000_000, bytes_accessed=20_000_000, transcendentals=0
        ),
    )(tab, near, *pieces)


def far_kernel(tab, far, basis, coefs, terms, p0, p1, p2, p3, cpart, cs, fx, fbuf, tbuf, sem, fsem):
    copy = pltpu.make_async_copy(coefs, cs, sem.at[0])
    copy.start()

    def far_copy(t):
        return pltpu.make_async_copy(far.at[:, tab[ORDER + t]], fbuf.at[t], fsem.at[0, t])

    def term_copy(t):
        return pltpu.make_async_copy(terms.at[tab[ORDER + t]], tbuf.at[t], fsem.at[1, t])

    for t in range(NBLK):
        far_copy(t).start()
        term_copy(t).start()
    copy.wait()
    for phase, ref in enumerate((p2, p1, p3, p0)):
        for q in range(4):
            t = phase * 4 + q
            row = tab[ORDER + t]
            used = tab[USED + row]
            for s in range(8):
                col = tab[FPOS + row * 8 + s]
                fx[q, pl.ds(s * K, K), :] = jnp.where(
                    s < used, cs[col], jnp.zeros((K, 2 * R), BF)
                )
            x = fx[q].T
            far_copy(t).wait()
            term_copy(t).wait()
            re = tbuf[t] + nn(x, fbuf[t, 0].reshape(B, B))
            acc = re + turn(nn(x, fbuf[t, 1].reshape(B, B)))
            pb = acc.astype(BF)
            ref[q] = acc if ref is p0 else pb
            cpart[row] = coef_of(basis[:, row], pb).astype(BF)


def far_terms(tab, far, basis, coefs, terms):
    anyspec = pl.BlockSpec(memory_space=pl.ANY)
    vmem = pl.BlockSpec(memory_space=pltpu.VMEM)
    outs = [jax.ShapeDtypeStruct(QUARTER, F32)] + [jax.ShapeDtypeStruct(QUARTER, BF)] * 3
    outs.append(jax.ShapeDtypeStruct((NBLK, K, 2 * R), BF))
    return pl.pallas_call(
        far_kernel,
        out_shape=outs,
        in_specs=[pl.BlockSpec(memory_space=pltpu.SMEM), anyspec, vmem, anyspec, anyspec],
        out_specs=[vmem] * len(outs),
        scratch_shapes=[
            pltpu.VMEM((512, K, 2 * R), BF),
            pltpu.VMEM((4, B, 2 * R), BF),
            pltpu.VMEM((NBLK, 2, 8, K, B), BF),
            pltpu.VMEM((NBLK, 2 * R, B), F32),
            pltpu.SemaphoreType.DMA((1,)),
            pltpu.SemaphoreType.DMA((2, NBLK)),
        ],
        compiler_params=pltpu.CompilerParams(vmem_limit_bytes=VMEM),
        cost_estimate=pl.CostEstimate(
            flops=2_000_000_000, bytes_accessed=13_000_000, transcendentals=0
        ),
    )(tab, far, basis, coefs, terms)


def both_kernel(sizes, coef, tab, near, far, basis, coefs, *refs):
    n = len(sizes)
    pieces = refs[:n]
    p0, p1, p2, p3 = refs[n : n + 4]
    cpart = refs[n + 4] if coef else None
    vt, cs, fx, nbuf, fbuf, vsem, csem, nsem, fsem = refs[n + 4 + coef :]

    def near_copy(t):
        return pltpu.make_async_copy(near.at[:, tab[ORDER + t]], nbuf.at[t], nsem.at[t])

    def far_copy(t):
        return pltpu.make_async_copy(far.at[:, tab[ORDER + t]], fbuf.at[t], fsem.at[t])

    copies = []
    for piece, size in zip(pieces, sizes):
        for b in range(size):
            m = len(copies)
            copies.append(pltpu.make_async_copy(piece.at[b], vt.at[tab[VSLOT + m]], vsem.at[m]))
    for c in copies:
        c.start()
    near_copy(0).start()
    whole = pltpu.make_async_copy(coefs, cs, csem.at[0])
    whole.start()
    far_copy(0).start()
    for t in range(1, LOOK):
        near_copy(t).start()
        far_copy(t).start()
    for c in copies:
        c.wait()

    for phase, ref in enumerate((p2, p1, p3, p0)):

        def body(h, carry, phase=phase, ref=ref):
            for u in range(2):
                q = h * 2 + u
                t = phase * 4 + q
                row = tab[ORDER + t]

                @pl.when(t < NBLK - LOOK)
                def _():
                    near_copy(t + LOOK).start()
                    far_copy(t + LOOK).start()

                near_copy(t).wait()
                re = jnp.zeros((2 * R, B), F32)
                im = jnp.zeros((2 * R, B), F32)
                for s in range(4):
                    x = vt[tab[NCOL + row * 4 + s]]
                    re = re + nt(x, nbuf[t, 0, s])
                    im = im + nt(x, nbuf[t, 1, s])
                if phase == 0 and u == 0:

                    @pl.when(h == 0)
                    def _():
                        whole.wait()

                far_copy(t).wait()
                used = tab[USED + row]
                for s in range(8):
                    col = tab[FPOS + row * 8 + s]
                    fx[u, pl.ds(s * K, K), :] = jnp.where(
                        s < used, cs[col], jnp.zeros((K, 2 * R), BF)
                    )
                x = fx[u].T
                re = re + nn(x, fbuf[t, 0].reshape(B, B))
                im = im + nn(x, fbuf[t, 1].reshape(B, B))
                acc = re + turn(im)
                pb = acc.astype(BF)
                ref[q] = acc if ref is p0 else pb
                if coef:
                    cpart[row] = coef_of(basis[:, row], pb).astype(BF)
            return carry

        lax.fori_loop(0, 2, body, 0)


def both_terms(tab, near, far, basis, coefs, pieces, coef):
    anyspec = pl.BlockSpec(memory_space=pl.ANY)
    vmem = pl.BlockSpec(memory_space=pltpu.VMEM)
    outs = [jax.ShapeDtypeStruct(QUARTER, F32)] + [jax.ShapeDtypeStruct(QUARTER, BF)] * 3
    if coef:
        outs.append(jax.ShapeDtypeStruct((NBLK, K, 2 * R), BF))
    sizes = [p.shape[0] for p in pieces]
    return pl.pallas_call(
        functools.partial(both_kernel, sizes, coef),
        out_shape=outs,
        in_specs=[pl.BlockSpec(memory_space=pltpu.SMEM), anyspec, anyspec, vmem]
        + [anyspec] * (1 + len(pieces)),
        out_specs=[vmem] * len(outs),
        scratch_shapes=[
            pltpu.VMEM((32, 2 * R, B), BF),
            pltpu.VMEM((512, K, 2 * R), BF),
            pltpu.VMEM((2, B, 2 * R), BF),
            pltpu.VMEM((NBLK, 2, 4, B, B), BF),
            pltpu.VMEM((NBLK, 2, 8, K, B), BF),
            pltpu.SemaphoreType.DMA((32,)),
            pltpu.SemaphoreType.DMA((1,)),
            pltpu.SemaphoreType.DMA((NBLK,)),
            pltpu.SemaphoreType.DMA((NBLK,)),
        ],
        compiler_params=pltpu.CompilerParams(vmem_limit_bytes=VMEM),
        cost_estimate=pl.CostEstimate(
            flops=10_000_000_000, bytes_accessed=30_000_000, transcendentals=0
        ),
    )(tab, near, far, basis, coefs, *pieces)


def gather_coef(c):
    return lax.all_gather(c, "rows", axis=0, tiled=True)


def gather_vector(v):
    beside = jnp.concatenate([send_row(v[2:], 1), send_row(v[:2], -1)], axis=0)
    mine = [v] + [send_x(v, d) for d in (1, 2, 3)]
    return mine + [beside] + [send_x(beside, d) for d in (1, 2, 3)]


def sum_x(own, parts):
    return (own + parts[1]) + (parts[0] + parts[2])


def all_sum(keep, give):
    m = keep + send_core(give)
    for bit in (1, 2):
        m = m + lax.ppermute(m, "cols", [(x, x ^ bit) for x in range(SIDE)])
    for bit in (2, 4, 8, 16):
        m = m + lax.ppermute(m, "rows", [(r, r ^ bit) for r in range(SIDE * SIDE * CORES)])
    return m, send_core(m)


HALVES = 5 * R // 4


def gram_kernel(core, f, g, e, keep, give, whole):
    def inner(a, b):
        acc = jnp.zeros((2 * R, 2 * R), F32)
        for q in range(4):
            acc = acc + nt(a[q], b[q], lax.Precision.HIGHEST)
        return acc[:R, :R] + acc[R:, R:]

    whole[:R, :R] = inner(g, f)
    whole[:R, R:] = inner(g, g)
    whole[R : 2 * R, :R] = inner(e, f)
    whole[R : 2 * R, R:] = inner(e, e)
    cross = inner(g, e)
    whole[2 * R :, :R] = cross[: R // 2]
    whole[2 * R :, R:] = cross[R // 2 :]
    k = core[0]
    keep[...] = whole[pl.ds(pl.multiple_of(k * HALVES, 8), HALVES), :]
    give[...] = whole[pl.ds(pl.multiple_of((1 - k) * HALVES, 8), HALVES), :]


def gram(core, f, g, e):
    vmem = pl.BlockSpec(memory_space=pltpu.VMEM)
    return pl.pallas_call(
        gram_kernel,
        in_specs=[pl.BlockSpec(memory_space=pltpu.SMEM), vmem, vmem, vmem],
        out_specs=[vmem, vmem],
        out_shape=[jax.ShapeDtypeStruct((HALVES, 2 * R), F32)] * 2,
        scratch_shapes=[pltpu.VMEM((2 * HALVES, 2 * R), F32)],
        compiler_params=pltpu.CompilerParams(vmem_limit_bytes=VMEM),
    )(core, f, g, e)


def both_halves(m):
    zero = jnp.zeros((R, R), m.dtype)
    return jnp.concatenate(
        [jnp.concatenate([m, zero], axis=1), jnp.concatenate([zero, m], axis=1)], axis=0
    )


def tn(a, b):
    return lax.dot_general(a, b, (((0,), (0,)), ((), ())), preferred_element_type=F32)


def solve(a):
    n = 2 * R
    eye = lax.broadcasted_iota(jnp.int32, (n, n), 0) == lax.broadcasted_iota(jnp.int32, (n, n), 1)
    diag = jnp.where(eye, a[:, :n], 0.0)
    down = lax.rsqrt(jnp.sum(diag, axis=1, keepdims=True))
    across = lax.rsqrt(jnp.sum(diag, axis=0, keepdims=True))
    a = a * down * jnp.concatenate([across, jnp.ones((1, n), F32)], axis=1)
    sub = lax.broadcasted_iota(jnp.int32, (8, 1), 0)
    groups = [a[i : i + 8] for i in range(0, 2 * R, 8)]
    for k in range(0, 2 * R, 2):
        g, j = k // 8, k % 8
        r0, r1 = groups[g][j : j + 1], groups[g][j + 1 : j + 2]
        d00, d01 = r0[:, k : k + 1], r0[:, k + 1 : k + 2]
        d10, d11 = r1[:, k : k + 1], r1[:, k + 1 : k + 2]
        scale = 1.0 / (d00 * d11 - d01 * d10)
        m0 = (r0 * d11 - r1 * d01) * scale
        m1 = (r1 * d00 - r0 * d10) * scale
        groups = [x - x[:, k : k + 1] * m0 - x[:, k + 1 : k + 2] * m1 for x in groups]
        groups[g] = jnp.where(sub == j, m0, jnp.where(sub == j + 1, m1, groups[g]))
    return jnp.concatenate(groups, axis=0)[:, n : n + R] * down


def update_kernel(info, half, other, guess, *refs):
    pieces, out = refs[:12], refs[12]
    whole, gbuf, buf, sem = refs[13:]
    copies = [pltpu.make_async_copy(guess, gbuf, sem.at[12])]
    copies += [pltpu.make_async_copy(p, buf.at[n], sem.at[n]) for n, p in enumerate(pieces)]
    for c in copies:
        c.start()
    core = info[4]
    whole[pl.ds(pl.multiple_of(core * HALVES, 8), HALVES), :] = half[...]
    whole[pl.ds(pl.multiple_of((1 - core) * HALVES, 8), HALVES), :] = other[...]
    cross = jnp.concatenate([whole[2 * R :, :R], whole[2 * R :, R:]], axis=0)
    zero = jnp.zeros((R, R), F32)
    upper = jnp.concatenate([whole[:R, R:], cross, whole[:R, :R], zero], axis=1)
    lower = jnp.concatenate([cross.T, whole[R : 2 * R, R:], whole[R : 2 * R, :R], zero], axis=1)
    y = solve(jnp.concatenate([upper, lower], axis=0))
    mats = []
    for m in (y[:R], y[R:]):
        high = m.astype(BF)
        mats.append((both_halves(high), both_halves((m - high.astype(F32)).astype(BF))))
    for c in copies:
        c.wait()
    for d in range(4):
        for q in range(4):
            at = pl.ds(pl.multiple_of((info[d] + 4 * q) * B, B), B)
            f, low, g = buf[d, q], buf[4 + d, q], buf[8 + d, q]
            acc = gbuf[at, :] + tn(f, mats[0][0]) + tn(f, mats[0][1]) + tn(low, mats[0][0])
            out[at, :] = acc + tn(g, mats[1][0]) + tn(g, mats[1][1])


def update(info, half, other, guess, f, low, g):
    vmem = pl.BlockSpec(memory_space=pltpu.VMEM)
    return pl.pallas_call(
        update_kernel,
        in_specs=[pl.BlockSpec(memory_space=pltpu.SMEM), vmem, vmem]
        + [pl.BlockSpec(memory_space=pl.ANY)] * 13,
        out_specs=vmem,
        out_shape=jax.ShapeDtypeStruct((NBLK * B, 2 * R), F32),
        scratch_shapes=[
            pltpu.VMEM((2 * HALVES, 2 * R), F32),
            pltpu.VMEM((NBLK * B, 2 * R), F32),
            pltpu.VMEM((12,) + QUARTER, BF),
            pltpu.SemaphoreType.DMA((13,)),
        ],
        compiler_params=pltpu.CompilerParams(vmem_limit_bytes=VMEM),
    )(info, half, other, guess, *f, *low, *g)


def summed(p0, p1, p2, p3):
    return sum_x(p0, [send_x(p, d).astype(F32) for d, p in ((1, p1), (2, p2), (3, p3))])


def summed_coef(cpart):
    return sum_x(cpart.astype(F32), [send_x(cpart, d).astype(F32) for d in (1, 2, 3)])


def shards(rhs, guess, near, near_cols, far_u, far_cols, far_count, basis):
    me_r = lax.axis_index("rows")
    me_c = lax.axis_index("cols")
    ints = lambda *v: jnp.array(v, jnp.int32)

    lane = jnp.arange(16, dtype=jnp.int32)
    order = (me_c + ints(2, 1, 3, 0)[lane // 4]) % SIDE + 4 * (lane % 4)
    ncol = (near_cols - (me_r * NBLK - HALF)).reshape(-1)
    fpos = far_cols.reshape(-1)
    used = jnp.clip(far_count - me_c * 8, 0, 8)
    e = (me_c - jnp.arange(4, dtype=jnp.int32)) % SIDE
    head = [order, ncol, fpos, used]
    slots_first = jnp.concatenate([HALF + lane, lane[:8], HALF + 16 + lane[:8]])
    four = (e[:, None] + ints(0, 4, 8, 12)).reshape(-1)
    beside = (e[:, None] + ints(0, 4, 24, 28)).reshape(-1)
    slots_next = jnp.concatenate([HALF + four, beside])
    tab_first = jnp.concatenate(head + [slots_first]).astype(jnp.int32)
    tab_next = jnp.concatenate(head + [slots_next]).astype(jnp.int32)

    whole = gather_coef(guess_coef(guess, basis))
    g_low, g_high, mine, c_diff = prepare(e, rhs, guess, basis)
    pieces = [g_low, g_high, send_row(g_high, 1), send_row(g_low, -1)]
    terms = near_terms(tab_first, near, pieces)
    p0, p1, p2, p3, cpart = far_terms(tab_first, far_u, basis, whole, terms)

    c_first = c_diff - summed_coef(cpart)
    whole = gather_coef(c_first.astype(BF))
    first = mine - summed(p0, p1, p2, p3)
    first_b = first.astype(BF)
    first_all = gather_vector(first_b)
    p0, p1, p2, p3, cpart = both_terms(tab_next, near, far_u, basis, whole, first_all, True)

    c_image = c_first + summed_coef(cpart)
    whole = gather_coef(c_image.astype(BF))
    image = first + summed(p0, p1, p2, p3)
    pieces = gather_vector(image.astype(BF))
    low = (first - lax.reduce_precision(first, 8, 7)).astype(BF)
    low_all = [low] + [send_x(low, d) for d in (1, 2, 3)]
    p0, p1, p2, p3 = both_terms(tab_next, near, far_u, basis, whole, pieces, False)
    p1, low_all = lax.optimization_barrier((p1, low_all))
    second = image + summed(p0, p1, p2, p3)

    core = me_r % CORES
    half, other = all_sum(*gram(core.reshape(1), first, image, second))
    info = jnp.concatenate([e, core.reshape(1)])
    return update(info, half, other, guess, first_all[:4], low_all, pieces[:4])


def solution(mesh):
    in_specs = (
        P("rows", None),
        P("rows", None),
        P(None, "rows", "cols", None, None),
        P("rows", "cols"),
        P(None, "rows", "cols", None, None),
        P("rows", "cols"),
        P("rows"),
        P(None, "rows", None, None),
    )
    return jax.shard_map(
        shards, mesh=mesh, in_specs=in_specs, out_specs=P("rows", None), check_vma=False
    )
```

```python
import functools

import jax
import jax.numpy as jnp
from jax import lax
from jax.experimental import pallas as pl
from jax.experimental.pallas import tpu as pltpu
from jax.sharding import PartitionSpec as P

B = 256
K = 32
R = 64
HALF = 8
SIDE = 4
CORES = 2
NBLK = 16
BF = jnp.bfloat16
F32 = jnp.float32


def row_id(z, y, k):
    return (z * SIDE + y) * CORES + k


def shift_y(d):
    return [
        (row_id(z, y, k), row_id(z, (y + d) % SIDE, k))
        for z in range(SIDE) for y in range(SIDE) for k in range(CORES)
    ]


def shift_z(d):
    return [
        (row_id(z, y, k), row_id((z + d) % SIDE, y, k))
        for z in range(SIDE) for y in range(SIDE) for k in range(CORES)
    ]


def send_x(a, d):
    return lax.ppermute(a, "cols", [(x, (x + d) % SIDE) for x in range(SIDE)])


def send_y(a, d):
    return lax.ppermute(a, "rows", shift_y(d))


def send_z(a, d):
    return lax.ppermute(a, "rows", shift_z(d))


def send_core(a):
    return lax.ppermute(a, "rows", [(r, r ^ 1) for r in range(SIDE * SIDE * CORES)])


def send_row(a, d):
    n = SIDE * SIDE * CORES
    return lax.ppermute(a, "rows", [(r, (r + d) % n) for r in range(n)])


def nn(a, b, precision=None):
    return lax.dot_general(
        a, b, (((1,), (0,)), ((), ())), preferred_element_type=F32, precision=precision
    )


def nt(a, b, precision=None):
    return lax.dot_general(
        a, b, (((1,), (1,)), ((), ())), preferred_element_type=F32, precision=precision
    )


def turn(x):
    return jnp.concatenate([-x[R:], x[:R]], axis=0)


def turn_lanes(x):
    return jnp.concatenate([-x[:, R:], x[:, :R]], axis=1)


def full_spec(shape):
    return pl.BlockSpec(shape, lambda *_: (0,) * len(shape))


ORDER, NCOL, FPOS, USED, VSLOT = 0, 16, 80, 208, 224
QUARTER = (4, 2 * R, B)
VMEM = 56 * 2 ** 20


def coef_of(basis, vec):
    both = nt(basis.reshape(2 * K, B), vec)
    return both[:K] + turn_lanes(both[K:])


def guess_coef_kernel(guess, basis, out):
    for i in range(NBLK):
        g = guess[pl.ds(i * B, B), :].astype(BF)
        both = nn(basis[:, i].reshape(2 * K, B), g)
        out[i] = (both[:K] + turn_lanes(both[K:])).astype(BF)


def guess_coef(guess, basis):
    return pl.pallas_call(
        guess_coef_kernel,
        out_shape=jax.ShapeDtypeStruct((NBLK, K, 2 * R), BF),
        compiler_params=pltpu.CompilerParams(vmem_limit_bytes=VMEM),
    )(guess, basis)


def prepare_kernel(tab, rhs, guess, basis, low, high, mine, cd):
    for i in range(NBLK):
        g = guess[pl.ds(i * B, B), :]
        (low if i < HALF else high)[i % HALF] = g.astype(BF).T
        d = (rhs[pl.ds(i * B, B), :] - g).astype(BF)
        both = nn(basis[:, i].reshape(2 * K, B), d)
        cd[i] = both[:K] + turn_lanes(both[K:])
    for q in range(4):
        at = pl.ds(pl.multiple_of((tab[0] + 4 * q) * B, B), B)
        mine[q] = (rhs[at, :] - guess[at, :]).T


def prepare(tab, rhs, guess, basis):
    vmem = pl.BlockSpec(memory_space=pltpu.VMEM)
    return pl.pallas_call(
        prepare_kernel,
        in_specs=[pl.BlockSpec(memory_space=pltpu.SMEM), vmem, vmem, vmem],
        out_specs=[vmem] * 4,
        out_shape=[
            jax.ShapeDtypeStruct((HALF, 2 * R, B), BF),
            jax.ShapeDtypeStruct((HALF, 2 * R, B), BF),
            jax.ShapeDtypeStruct(QUARTER, F32),
            jax.ShapeDtypeStruct((NBLK, K, 2 * R), F32),
        ],
        compiler_params=pltpu.CompilerParams(vmem_limit_bytes=VMEM),
    )(tab, rhs, guess, basis)


LOOK = 3


def near_kernel(sizes, first, groups, tab, near, *refs):
    n, m = len(sizes), len(groups)
    pieces, outs = refs[:n], refs[n : n + m]
    turned = refs[n + m] if first else None
    vt, nbuf, vsem, nsem = refs[n + m + first : n + m + 4 + first]
    tbuf, tsem = refs[n + m + 5 :] if first else (None, None)
    steps = range(4 * groups[0], 4 * groups[0] + 4 * m)

    def near_copy(t):
        source = near.at[:, tab[ORDER + t]] if first else near.at[t]
        return pltpu.make_async_copy(source, nbuf.at[t - steps[0]], nsem.at[t - steps[0]])

    def turned_copy(t):
        return pltpu.make_async_copy(tbuf.at[t], turned.at[t], tsem.at[t])

    copies = []
    for piece, size in zip(pieces, sizes):
        for b in range(size):
            i = len(copies)
            copies.append(pltpu.make_async_copy(piece.at[b], vt.at[tab[VSLOT + i]], vsem.at[i]))
    for c in copies:
        c.start()
    for t in steps[:LOOK]:
        near_copy(t).start()
    for c in copies:
        c.wait()
    for t in steps:
        if t + LOOK in steps:
            near_copy(t + LOOK).start()
        near_copy(t).wait()
        row = tab[ORDER + t]
        re = jnp.zeros((2 * R, B), F32)
        im = jnp.zeros((2 * R, B), F32)
        for s in range(4):
            x = vt[tab[NCOL + row * 4 + s]]
            a, b = nbuf[t - steps[0], 0, s], nbuf[t - steps[0], 1, s]
            if first:
                a, b = a.T, b.T
                tbuf[t, 0, s] = a
                tbuf[t, 1, s] = b
            re = re + nn(x, a)
            im = im + nn(x, b)
        if first:
            turned_copy(t).start()
        out = outs[t // 4 - groups[0]]
        out[t % 4] = (re + turn(im)).astype(out.dtype)
    if first:
        for t in steps:
            turned_copy(t).wait()


def near_terms(tab, near, pieces, first, groups):
    anyspec = pl.BlockSpec(memory_space=pl.ANY)
    vmem = pl.BlockSpec(memory_space=pltpu.VMEM)
    sizes = [p.shape[0] for p in pieces]
    count = 4 * len(groups)
    held = (count, 2, 4, B, B)
    scratch = [
        pltpu.VMEM((32, 2 * R, B), BF),
        pltpu.VMEM(held, BF),
        pltpu.SemaphoreType.DMA((32,)),
        pltpu.SemaphoreType.DMA((count,)),
    ]
    if first:
        scratch += [pltpu.VMEM(held, BF), pltpu.SemaphoreType.DMA((count,))]
    outs = [jax.ShapeDtypeStruct(QUARTER, F32 if g == 3 else BF) for g in groups]
    return pl.pallas_call(
        functools.partial(near_kernel, sizes, first, groups),
        out_shape=outs + [jax.ShapeDtypeStruct(held, BF)] * first,
        in_specs=[pl.BlockSpec(memory_space=pltpu.SMEM)] + [anyspec] * (1 + len(pieces)),
        out_specs=[vmem] * len(groups) + [anyspec] * first,
        scratch_shapes=scratch,
        compiler_params=pltpu.CompilerParams(vmem_limit_bytes=VMEM),
        cost_estimate=pl.CostEstimate(
            flops=2_000_000_000 * len(groups),
            bytes_accessed=5_000_000 * len(groups),
            transcendentals=0,
        ),
    )(tab, near, *pieces)


def far_part_kernel(tab, far, basis, coefs, t0, t1, t2, t3, p0, p1, p2, p3, cpart, cs, fx, fbuf, sem, fsem):
    copy = pltpu.make_async_copy(coefs, cs, sem.at[0])
    copy.start()

    def far_copy(t):
        return pltpu.make_async_copy(far.at[:, tab[ORDER + t]], fbuf.at[t], fsem.at[t])

    for t in range(NBLK):
        far_copy(t).start()
    copy.wait()
    for phase, (terms, ref) in enumerate(((t2, p2), (t1, p1), (t3, p3), (t0, p0))):
        for q in range(4):
            t = phase * 4 + q
            row = tab[ORDER + t]
            used = tab[USED + row]
            for s in range(8):
                col = tab[FPOS + row * 8 + s]
                fx[q, pl.ds(s * K, K), :] = jnp.where(
                    s < used, cs[col], jnp.zeros((K, 2 * R), BF)
                )
            x = fx[q].T
            far_copy(t).wait()
            re = terms[q].astype(F32) + nn(x, fbuf[t, 0].reshape(B, B))
            acc = re + turn(nn(x, fbuf[t, 1].reshape(B, B)))
            pb = acc.astype(BF)
            ref[q] = acc if ref is p0 else pb
            cpart[row] = coef_of(basis[:, row], pb).astype(BF)


def far_part(tab, far, basis, coefs, terms):
    anyspec = pl.BlockSpec(memory_space=pl.ANY)
    vmem = pl.BlockSpec(memory_space=pltpu.VMEM)
    smem = pl.BlockSpec(memory_space=pltpu.SMEM)
    outs = [jax.ShapeDtypeStruct(QUARTER, F32)] + [jax.ShapeDtypeStruct(QUARTER, BF)] * 3
    outs.append(jax.ShapeDtypeStruct((NBLK, K, 2 * R), BF))
    return pl.pallas_call(
        far_part_kernel,
        out_shape=outs,
        in_specs=[smem, anyspec, vmem, anyspec] + [vmem] * 4,
        out_specs=[vmem] * len(outs),
        scratch_shapes=[
            pltpu.VMEM((512, K, 2 * R), BF),
            pltpu.VMEM((4, B, 2 * R), BF),
            pltpu.VMEM((NBLK, 2, 8, K, B), BF),
            pltpu.SemaphoreType.DMA((1,)),
            pltpu.SemaphoreType.DMA((NBLK,)),
        ],
        compiler_params=pltpu.CompilerParams(vmem_limit_bytes=VMEM),
        cost_estimate=pl.CostEstimate(
            flops=2_000_000_000, bytes_accessed=13_000_000, transcendentals=0
        ),
    )(tab, far, basis, coefs, *terms)


def both_kernel(sizes, coef, tab, turned, far, basis, coefs, *refs):
    n = len(sizes)
    pieces = refs[:n]
    p0, p1, p2, p3 = refs[n : n + 4]
    cpart = refs[n + 4] if coef else None
    vt, cs, fx, ahead, nbuf, fbuf, vsem, csem, nsem, fsem = refs[n + 4 + coef :]

    def near_copy(t):
        return pltpu.make_async_copy(turned.at[t], nbuf.at[t], nsem.at[t])

    def far_copy(t):
        return pltpu.make_async_copy(far.at[:, tab[ORDER + t]], fbuf.at[t], fsem.at[t])

    copies = []
    for piece, size in zip(pieces, sizes):
        for b in range(size):
            m = len(copies)
            copies.append(pltpu.make_async_copy(piece.at[b], vt.at[tab[VSLOT + m]], vsem.at[m]))
    for c in copies:
        c.start()
    near_copy(0).start()
    near_copy(1).start()
    whole = pltpu.make_async_copy(coefs, cs, csem.at[0])
    for c in copies:
        c.wait()
    whole.start()
    near_copy(2).start()
    near_copy(3).start()
    far_copy(0).start()
    far_copy(1).start()

    def near_part(t):
        near_copy(t).wait()
        row = tab[ORDER + t]
        re = jnp.zeros((2 * R, B), F32)
        im = jnp.zeros((2 * R, B), F32)
        for s in range(4):
            x = vt[tab[NCOL + row * 4 + s]]
            re = re + nn(x, nbuf[t, 0, s])
            im = im + nn(x, nbuf[t, 1, s])
        return re + turn(im)

    for t in range(4):
        ahead[t] = near_part(t)
        near_copy(t + 4).start()
        if t >= 2:
            far_copy(t).start()
    whole.wait()
    for t in range(NBLK):
        if t + 4 < NBLK:
            if t + 8 < NBLK and t < 12:
                near_copy(t + 8).start()
            far_copy(t + 4).start()
        terms = ahead[t] if t < 4 else near_part(t)
        row = tab[ORDER + t]
        used = tab[USED + row]
        for s in range(8):
            col = tab[FPOS + row * 8 + s]
            fx[t % 4, pl.ds(s * K, K), :] = jnp.where(
                s < used, cs[col], jnp.zeros((K, 2 * R), BF)
            )
        x = fx[t % 4].T
        far_copy(t).wait()
        re = terms + nn(x, fbuf[t, 0].reshape(B, B))
        acc = re + turn(nn(x, fbuf[t, 1].reshape(B, B)))
        pb = acc.astype(BF)
        ref = (p2, p1, p3, p0)[t // 4]
        ref[t % 4] = acc if ref is p0 else pb
        if coef:
            cpart[row] = coef_of(basis[:, row], pb).astype(BF)


def both_terms(tab, near, far, basis, coefs, pieces, coef):
    anyspec = pl.BlockSpec(memory_space=pl.ANY)
    vmem = pl.BlockSpec(memory_space=pltpu.VMEM)
    outs = [jax.ShapeDtypeStruct(QUARTER, F32)] + [jax.ShapeDtypeStruct(QUARTER, BF)] * 3
    if coef:
        outs.append(jax.ShapeDtypeStruct((NBLK, K, 2 * R), BF))
    sizes = [p.shape[0] for p in pieces]
    return pl.pallas_call(
        functools.partial(both_kernel, sizes, coef),
        out_shape=outs,
        in_specs=[pl.BlockSpec(memory_space=pltpu.SMEM), anyspec, anyspec, vmem]
        + [anyspec] * (1 + len(pieces)),
        out_specs=[vmem] * len(outs),
        scratch_shapes=[
            pltpu.VMEM((32, 2 * R, B), BF),
            pltpu.VMEM((512, K, 2 * R), BF),
            pltpu.VMEM((4, B, 2 * R), BF),
            pltpu.VMEM(QUARTER, F32),
            pltpu.VMEM((NBLK, 2, 4, B, B), BF),
            pltpu.VMEM((NBLK, 2, 8, K, B), BF),
            pltpu.SemaphoreType.DMA((32,)),
            pltpu.SemaphoreType.DMA((1,)),
            pltpu.SemaphoreType.DMA((NBLK,)),
            pltpu.SemaphoreType.DMA((NBLK,)),
        ],
        compiler_params=pltpu.CompilerParams(vmem_limit_bytes=VMEM),
        cost_estimate=pl.CostEstimate(
            flops=10_000_000_000, bytes_accessed=30_000_000, transcendentals=0
        ),
    )(tab, near, far, basis, coefs, *pieces)


def gather_coef(c):
    return lax.all_gather(c, "rows", axis=0, tiled=True)


def gather_vector(v):
    beside = jnp.concatenate([send_row(v[2:], 1), send_row(v[:2], -1)], axis=0)
    mine = [v] + [send_x(v, d) for d in (1, 2, 3)]
    return mine + [beside] + [send_x(beside, d) for d in (1, 2, 3)]


def sum_x(own, parts):
    return (own + parts[1]) + (parts[0] + parts[2])


def all_sum(keep, give):
    m = keep + send_core(give)
    for bit in (1, 2):
        m = m + lax.ppermute(m, "cols", [(x, x ^ bit) for x in range(SIDE)])
    for bit in (2, 4, 8, 16):
        m = m + lax.ppermute(m, "rows", [(r, r ^ bit) for r in range(SIDE * SIDE * CORES)])
    return m, send_core(m)


HALVES = 5 * R // 4


def gram_kernel(core, f, g, e, keep, give, whole):
    def inner(a, b):
        acc = jnp.zeros((2 * R, 2 * R), F32)
        for q in range(4):
            acc = acc + nt(a[q], b[q], lax.Precision.HIGHEST)
        return acc[:R, :R] + acc[R:, R:]

    whole[:R, :R] = inner(g, f)
    whole[:R, R:] = inner(g, g)
    whole[R : 2 * R, :R] = inner(e, f)
    whole[R : 2 * R, R:] = inner(e, e)
    cross = inner(g, e)
    whole[2 * R :, :R] = cross[: R // 2]
    whole[2 * R :, R:] = cross[R // 2 :]
    k = core[0]
    keep[...] = whole[pl.ds(pl.multiple_of(k * HALVES, 8), HALVES), :]
    give[...] = whole[pl.ds(pl.multiple_of((1 - k) * HALVES, 8), HALVES), :]


def gram(core, f, g, e):
    vmem = pl.BlockSpec(memory_space=pltpu.VMEM)
    return pl.pallas_call(
        gram_kernel,
        in_specs=[pl.BlockSpec(memory_space=pltpu.SMEM), vmem, vmem, vmem],
        out_specs=[vmem, vmem],
        out_shape=[jax.ShapeDtypeStruct((HALVES, 2 * R), F32)] * 2,
        scratch_shapes=[pltpu.VMEM((2 * HALVES, 2 * R), F32)],
        compiler_params=pltpu.CompilerParams(vmem_limit_bytes=VMEM),
    )(core, f, g, e)


def both_halves(m):
    zero = jnp.zeros((R, R), m.dtype)
    return jnp.concatenate(
        [jnp.concatenate([m, zero], axis=1), jnp.concatenate([zero, m], axis=1)], axis=0
    )


def tn(a, b):
    return lax.dot_general(a, b, (((0,), (0,)), ((), ())), preferred_element_type=F32)


def solve(a):
    n = 2 * R
    eye = lax.broadcasted_iota(jnp.int32, (n, n), 0) == lax.broadcasted_iota(jnp.int32, (n, n), 1)
    diag = jnp.where(eye, a[:, :n], 0.0)
    down = lax.rsqrt(jnp.sum(diag, axis=1, keepdims=True))
    across = lax.rsqrt(jnp.sum(diag, axis=0, keepdims=True))
    a = a * down * jnp.concatenate([across, jnp.ones((1, n), F32)], axis=1)
    sub = lax.broadcasted_iota(jnp.int32, (8, 1), 0)
    groups = [a[i : i + 8] for i in range(0, 2 * R, 8)]
    for k in range(0, 2 * R, 2):
        g, j = k // 8, k % 8
        r0, r1 = groups[g][j : j + 1], groups[g][j + 1 : j + 2]
        d00, d01 = r0[:, k : k + 1], r0[:, k + 1 : k + 2]
        d10, d11 = r1[:, k : k + 1], r1[:, k + 1 : k + 2]
        scale = 1.0 / (d00 * d11 - d01 * d10)
        m0 = (r0 * d11 - r1 * d01) * scale
        m1 = (r1 * d00 - r0 * d10) * scale
        groups = [x - x[:, k : k + 1] * m0 - x[:, k + 1 : k + 2] * m1 for x in groups]
        groups[g] = jnp.where(sub == j, m0, jnp.where(sub == j + 1, m1, groups[g]))
    return jnp.concatenate(groups, axis=0)[:, n : n + R] * down


def update_kernel(info, half, other, guess, *refs):
    pieces, out = refs[:12], refs[12]
    whole, gbuf, buf, sem = refs[13:]
    copies = [pltpu.make_async_copy(guess, gbuf, sem.at[12])]
    copies += [pltpu.make_async_copy(p, buf.at[n], sem.at[n]) for n, p in enumerate(pieces)]
    for c in copies:
        c.start()
    core = info[4]
    whole[pl.ds(pl.multiple_of(core * HALVES, 8), HALVES), :] = half[...]
    whole[pl.ds(pl.multiple_of((1 - core) * HALVES, 8), HALVES), :] = other[...]
    cross = jnp.concatenate([whole[2 * R :, :R], whole[2 * R :, R:]], axis=0)
    zero = jnp.zeros((R, R), F32)
    upper = jnp.concatenate([whole[:R, R:], cross, whole[:R, :R], zero], axis=1)
    lower = jnp.concatenate([cross.T, whole[R : 2 * R, R:], whole[R : 2 * R, :R], zero], axis=1)
    y = solve(jnp.concatenate([upper, lower], axis=0))
    mats = []
    for m in (y[:R], y[R:]):
        high = m.astype(BF)
        mats.append((both_halves(high), both_halves((m - high.astype(F32)).astype(BF))))
    for c in copies:
        c.wait()
    for d in range(4):
        for q in range(4):
            at = pl.ds(pl.multiple_of((info[d] + 4 * q) * B, B), B)
            f, low, g = buf[d, q], buf[4 + d, q], buf[8 + d, q]
            acc = gbuf[at, :] + tn(f, mats[0][0]) + tn(f, mats[0][1]) + tn(low, mats[0][0])
            out[at, :] = acc + tn(g, mats[1][0]) + tn(g, mats[1][1])


def update(info, half, other, guess, f, low, g):
    vmem = pl.BlockSpec(memory_space=pltpu.VMEM)
    return pl.pallas_call(
        update_kernel,
        in_specs=[pl.BlockSpec(memory_space=pltpu.SMEM), vmem, vmem]
        + [pl.BlockSpec(memory_space=pl.ANY)] * 13,
        out_specs=vmem,
        out_shape=jax.ShapeDtypeStruct((NBLK * B, 2 * R), F32),
        scratch_shapes=[
            pltpu.VMEM((2 * HALVES, 2 * R), F32),
            pltpu.VMEM((NBLK * B, 2 * R), F32),
            pltpu.VMEM((12,) + QUARTER, BF),
            pltpu.SemaphoreType.DMA((13,)),
        ],
        compiler_params=pltpu.CompilerParams(vmem_limit_bytes=VMEM),
    )(info, half, other, guess, *f, *low, *g)


def summed(p0, p1, p2, p3):
    return sum_x(p0, [send_x(p, d).astype(F32) for d, p in ((1, p1), (2, p2), (3, p3))])


def summed_coef(cpart):
    return sum_x(cpart.astype(F32), [send_x(cpart, d).astype(F32) for d in (1, 2, 3)])


def shards(rhs, guess, near, near_cols, far_u, far_cols, far_count, basis):
    me_r = lax.axis_index("rows")
    me_c = lax.axis_index("cols")
    ints = lambda *v: jnp.array(v, jnp.int32)

    lane = jnp.arange(16, dtype=jnp.int32)
    order = (me_c + ints(2, 1, 3, 0)[lane // 4]) % SIDE + 4 * (lane % 4)
    ncol = (near_cols - (me_r * NBLK - HALF)).reshape(-1)
    fpos = far_cols.reshape(-1)
    used = jnp.clip(far_count - me_c * 8, 0, 8)
    e = (me_c - jnp.arange(4, dtype=jnp.int32)) % SIDE
    head = [order, ncol, fpos, used]
    slots_first = jnp.concatenate([HALF + lane, lane[:8], HALF + 16 + lane[:8]])
    four = (e[:, None] + ints(0, 4, 8, 12)).reshape(-1)
    beside = (e[:, None] + ints(0, 4, 24, 28)).reshape(-1)
    slots_next = jnp.concatenate([HALF + four, beside])
    tab_first = jnp.concatenate(head + [slots_first]).astype(jnp.int32)
    tab_next = jnp.concatenate(head + [slots_next]).astype(jnp.int32)

    whole = gather_coef(guess_coef(guess, basis))
    g_low, g_high, mine, c_diff = prepare(e, rhs, guess, basis)
    pieces = [g_low, g_high, send_row(g_high, 1), send_row(g_low, -1)]
    p2, p1, p3, p0, turned = near_terms(tab_first, near, pieces, True, (0, 1, 2, 3))
    p0, p1, p2, p3, cpart = far_part(tab_first, far_u, basis, whole, [p0, p1, p2, p3])

    c_first = c_diff - summed_coef(cpart)
    whole = gather_coef(c_first.astype(BF))
    first = mine - summed(p0, p1, p2, p3)
    first_b = first.astype(BF)
    first_all = gather_vector(first_b)
    p0, p1, p2, p3, cpart = both_terms(tab_next, turned, far_u, basis, whole, first_all, True)

    c_image = c_first + summed_coef(cpart)
    whole = gather_coef(c_image.astype(BF))
    image = first + summed(p0, p1, p2, p3)
    pieces = gather_vector(image.astype(BF))
    low = (first - lax.reduce_precision(first, 8, 7)).astype(BF)
    low_all = [low] + [send_x(low, d) for d in (1, 2, 3)]
    p0, p1, p2, p3 = both_terms(tab_next, turned, far_u, basis, whole, pieces, False)
    p1, low_all = lax.optimization_barrier((p1, low_all))
    second = image + summed(p0, p1, p2, p3)

    core = me_r % CORES
    half, other = all_sum(*gram(core.reshape(1), first, image, second))
    info = jnp.concatenate([e, core.reshape(1)])
    return update(info, half, other, guess, first_all[:4], low_all, pieces[:4])


def solution(mesh):
    in_specs = (
        P("rows", None),
        P("rows", None),
        P(None, "rows", "cols", None, None),
        P("rows", "cols"),
        P(None, "rows", "cols", None, None),
        P("rows", "cols"),
        P("rows"),
        P(None, "rows", None, None),
    )
    return jax.shard_map(
        shards, mesh=mesh, in_specs=in_specs, out_specs=P("rows", None), check_vma=False
    )
```

```python
import functools

import jax
import jax.numpy as jnp
from jax import lax
from jax.experimental import pallas as pl
from jax.experimental.pallas import tpu as pltpu
from jax.sharding import PartitionSpec as P

B = 256
K = 32
R = 64
HALF = 8
SIDE = 4
CORES = 2
NBLK = 16
BF = jnp.bfloat16
F32 = jnp.float32


def row_id(z, y, k):
    return (z * SIDE + y) * CORES + k


def shift_y(d):
    return [
        (row_id(z, y, k), row_id(z, (y + d) % SIDE, k))
        for z in range(SIDE) for y in range(SIDE) for k in range(CORES)
    ]


def shift_z(d):
    return [
        (row_id(z, y, k), row_id((z + d) % SIDE, y, k))
        for z in range(SIDE) for y in range(SIDE) for k in range(CORES)
    ]


def send_x(a, d):
    return lax.ppermute(a, "cols", [(x, (x + d) % SIDE) for x in range(SIDE)])


def send_y(a, d):
    return lax.ppermute(a, "rows", shift_y(d))


def send_z(a, d):
    return lax.ppermute(a, "rows", shift_z(d))


def send_core(a):
    return lax.ppermute(a, "rows", [(r, r ^ 1) for r in range(SIDE * SIDE * CORES)])


def send_row(a, d):
    n = SIDE * SIDE * CORES
    return lax.ppermute(a, "rows", [(r, (r + d) % n) for r in range(n)])


def nn(a, b, precision=None):
    return lax.dot_general(
        a, b, (((1,), (0,)), ((), ())), preferred_element_type=F32, precision=precision
    )


def nt(a, b, precision=None):
    return lax.dot_general(
        a, b, (((1,), (1,)), ((), ())), preferred_element_type=F32, precision=precision
    )


def turn(x):
    return jnp.concatenate([-x[R:], x[:R]], axis=0)


def turn_lanes(x):
    return jnp.concatenate([-x[:, R:], x[:, :R]], axis=1)


def full_spec(shape):
    return pl.BlockSpec(shape, lambda *_: (0,) * len(shape))


ORDER, NCOL, FPOS, USED, VSLOT = 0, 16, 80, 208, 224
QUARTER = (4, 2 * R, B)
VMEM = 56 * 2 ** 20


def coef_of(basis, vec):
    both = nt(basis.reshape(2 * K, B), vec)
    return both[:K] + turn_lanes(both[K:])


def guess_coef_kernel(guess, basis, out):
    for i in range(NBLK):
        g = guess[pl.ds(i * B, B), :].astype(BF)
        both = nn(basis[:, i].reshape(2 * K, B), g)
        out[i] = (both[:K] + turn_lanes(both[K:])).astype(BF)


def guess_coef(guess, basis):
    return pl.pallas_call(
        guess_coef_kernel,
        out_shape=jax.ShapeDtypeStruct((NBLK, K, 2 * R), BF),
        compiler_params=pltpu.CompilerParams(vmem_limit_bytes=VMEM),
    )(guess, basis)


def prepare_kernel(tab, rhs, guess, basis, low, high, mine, cd):
    for i in range(NBLK):
        g = guess[pl.ds(i * B, B), :]
        (low if i < HALF else high)[i % HALF] = g.astype(BF).T
        d = (rhs[pl.ds(i * B, B), :] - g).astype(BF)
        both = nn(basis[:, i].reshape(2 * K, B), d)
        cd[i] = both[:K] + turn_lanes(both[K:])
    for q in range(4):
        at = pl.ds(pl.multiple_of((tab[0] + 4 * q) * B, B), B)
        mine[q] = (rhs[at, :] - guess[at, :]).T


def prepare(tab, rhs, guess, basis):
    vmem = pl.BlockSpec(memory_space=pltpu.VMEM)
    return pl.pallas_call(
        prepare_kernel,
        in_specs=[pl.BlockSpec(memory_space=pltpu.SMEM), vmem, vmem, vmem],
        out_specs=[vmem] * 4,
        out_shape=[
            jax.ShapeDtypeStruct((HALF, 2 * R, B), BF),
            jax.ShapeDtypeStruct((HALF, 2 * R, B), BF),
            jax.ShapeDtypeStruct(QUARTER, F32),
            jax.ShapeDtypeStruct((NBLK, K, 2 * R), F32),
        ],
        compiler_params=pltpu.CompilerParams(vmem_limit_bytes=VMEM),
    )(tab, rhs, guess, basis)


LOOK = 3


def near_kernel(sizes, first, groups, tab, near, *refs):
    n, m = len(sizes), len(groups)
    pieces, outs = refs[:n], refs[n : n + m]
    turned = refs[n + m] if first else None
    vt, nbuf, vsem, nsem = refs[n + m + first : n + m + 4 + first]
    tbuf, tsem = refs[n + m + 5 :] if first else (None, None)
    steps = range(4 * groups[0], 4 * groups[0] + 4 * m)

    def near_copy(t):
        source = near.at[:, tab[ORDER + t]] if first else near.at[t]
        return pltpu.make_async_copy(source, nbuf.at[t - steps[0]], nsem.at[t - steps[0]])

    def turned_copy(t):
        return pltpu.make_async_copy(tbuf.at[t], turned.at[t], tsem.at[t])

    copies = []
    for piece, size in zip(pieces, sizes):
        for b in range(size):
            i = len(copies)
            copies.append(pltpu.make_async_copy(piece.at[b], vt.at[tab[VSLOT + i]], vsem.at[i]))
    for c in copies:
        c.start()
    for t in steps[:LOOK]:
        near_copy(t).start()
    for c in copies:
        c.wait()
    for t in steps:
        if t + LOOK in steps:
            near_copy(t + LOOK).start()
        near_copy(t).wait()
        row = tab[ORDER + t]
        re = jnp.zeros((2 * R, B), F32)
        im = jnp.zeros((2 * R, B), F32)
        for s in range(4):
            x = vt[tab[NCOL + row * 4 + s]]
            a, b = nbuf[t - steps[0], 0, s], nbuf[t - steps[0], 1, s]
            if first:
                a, b = a.T, b.T
                tbuf[t, 0, s] = a
                tbuf[t, 1, s] = b
            re = re + nn(x, a)
            im = im + nn(x, b)
        if first:
            turned_copy(t).start()
        out = outs[t // 4 - groups[0]]
        out[t % 4] = (re + turn(im)).astype(out.dtype)
    if first:
        for t in steps:
            turned_copy(t).wait()


def near_terms(tab, near, pieces, first, groups):
    anyspec = pl.BlockSpec(memory_space=pl.ANY)
    vmem = pl.BlockSpec(memory_space=pltpu.VMEM)
    sizes = [p.shape[0] for p in pieces]
    count = 4 * len(groups)
    held = (count, 2, 4, B, B)
    scratch = [
        pltpu.VMEM((32, 2 * R, B), BF),
        pltpu.VMEM(held, BF),
        pltpu.SemaphoreType.DMA((32,)),
        pltpu.SemaphoreType.DMA((count,)),
    ]
    if first:
        scratch += [pltpu.VMEM(held, BF), pltpu.SemaphoreType.DMA((count,))]
    outs = [jax.ShapeDtypeStruct(QUARTER, F32 if g == 3 else BF) for g in groups]
    return pl.pallas_call(
        functools.partial(near_kernel, sizes, first, groups),
        out_shape=outs + [jax.ShapeDtypeStruct(held, BF)] * first,
        in_specs=[pl.BlockSpec(memory_space=pltpu.SMEM)] + [anyspec] * (1 + len(pieces)),
        out_specs=[vmem] * len(groups) + [anyspec] * first,
        scratch_shapes=scratch,
        compiler_params=pltpu.CompilerParams(vmem_limit_bytes=VMEM),
        cost_estimate=pl.CostEstimate(
            flops=2_000_000_000 * len(groups),
            bytes_accessed=5_000_000 * len(groups),
            transcendentals=0,
        ),
    )(tab, near, *pieces)


def far_part_kernel(tab, far, basis, coefs, t0, t1, t2, t3, p0, p1, p2, p3, cpart, cs, fx, fbuf, sem, fsem):
    copy = pltpu.make_async_copy(coefs, cs, sem.at[0])
    copy.start()

    def far_copy(t):
        return pltpu.make_async_copy(far.at[:, tab[ORDER + t]], fbuf.at[t], fsem.at[t])

    for t in range(4):
        far_copy(t).start()
    copy.wait()
    for t in range(4, NBLK):
        far_copy(t).start()
    for phase, (terms, ref) in enumerate(((t2, p2), (t1, p1), (t3, p3), (t0, p0))):
        for q in range(4):
            t = phase * 4 + q
            row = tab[ORDER + t]
            used = tab[USED + row]
            for s in range(8):
                col = tab[FPOS + row * 8 + s]
                fx[q, pl.ds(s * K, K), :] = jnp.where(
                    s < used, cs[col], jnp.zeros((K, 2 * R), BF)
                )
            x = fx[q].T
            far_copy(t).wait()
            re = terms[q].astype(F32) + nn(x, fbuf[t, 0].reshape(B, B))
            acc = re + turn(nn(x, fbuf[t, 1].reshape(B, B)))
            pb = acc.astype(BF)
            ref[q] = acc if ref is p0 else pb
            cpart[row] = coef_of(basis[:, row], pb).astype(BF)


def far_part(tab, far, basis, coefs, terms):
    anyspec = pl.BlockSpec(memory_space=pl.ANY)
    vmem = pl.BlockSpec(memory_space=pltpu.VMEM)
    smem = pl.BlockSpec(memory_space=pltpu.SMEM)
    outs = [jax.ShapeDtypeStruct(QUARTER, F32)] + [jax.ShapeDtypeStruct(QUARTER, BF)] * 3
    outs.append(jax.ShapeDtypeStruct((NBLK, K, 2 * R), BF))
    return pl.pallas_call(
        far_part_kernel,
        out_shape=outs,
        in_specs=[smem, anyspec, vmem, anyspec] + [vmem] * 4,
        out_specs=[vmem] * len(outs),
        scratch_shapes=[
            pltpu.VMEM((512, K, 2 * R), BF),
            pltpu.VMEM((4, B, 2 * R), BF),
            pltpu.VMEM((NBLK, 2, 8, K, B), BF),
            pltpu.SemaphoreType.DMA((1,)),
            pltpu.SemaphoreType.DMA((NBLK,)),
        ],
        compiler_params=pltpu.CompilerParams(vmem_limit_bytes=VMEM),
        cost_estimate=pl.CostEstimate(
            flops=2_000_000_000, bytes_accessed=13_000_000, transcendentals=0
        ),
    )(tab, far, basis, coefs, *terms)


def both_kernel(sizes, coef, tab, turned, far, basis, coefs, *refs):
    n = len(sizes)
    pieces = refs[:n]
    p0, p1, p2, p3 = refs[n : n + 4]
    cpart = refs[n + 4] if coef else None
    vt, cs, fx, ahead, nbuf, fbuf, vsem, csem, nsem, fsem = refs[n + 4 + coef :]

    def near_copy(t):
        return pltpu.make_async_copy(turned.at[t], nbuf.at[t], nsem.at[t])

    def far_copy(t):
        return pltpu.make_async_copy(far.at[:, tab[ORDER + t]], fbuf.at[t], fsem.at[t])

    copies = []
    for piece, size in zip(pieces, sizes):
        for b in range(size):
            m = len(copies)
            copies.append(pltpu.make_async_copy(piece.at[b], vt.at[tab[VSLOT + m]], vsem.at[m]))
    for c in copies:
        c.start()
    near_copy(0).start()
    near_copy(1).start()
    whole = pltpu.make_async_copy(coefs, cs, csem.at[0])
    for c in copies:
        c.wait()
    whole.start()
    near_copy(2).start()
    near_copy(3).start()
    far_copy(0).start()
    far_copy(1).start()

    def near_part(t):
        near_copy(t).wait()
        row = tab[ORDER + t]
        re = jnp.zeros((2 * R, B), F32)
        im = jnp.zeros((2 * R, B), F32)
        for s in range(4):
            x = vt[tab[NCOL + row * 4 + s]]
            re = re + nn(x, nbuf[t, 0, s])
            im = im + nn(x, nbuf[t, 1, s])
        return re + turn(im)

    for t in range(4):
        ahead[t] = near_part(t)
        near_copy(t + 4).start()
        if t >= 2:
            far_copy(t).start()
    whole.wait()
    for t in range(NBLK):
        if t + 4 < NBLK:
            if t + 8 < NBLK and t < 12:
                near_copy(t + 8).start()
            far_copy(t + 4).start()
        terms = ahead[t] if t < 4 else near_part(t)
        if coef and t:
            cpart[row] = coef_of(basis[:, row], pb).astype(BF)
        row = tab[ORDER + t]
        used = tab[USED + row]
        for s in range(8):
            col = tab[FPOS + row * 8 + s]
            fx[t % 4, pl.ds(s * K, K), :] = jnp.where(
                s < used, cs[col], jnp.zeros((K, 2 * R), BF)
            )
        x = fx[t % 4].T
        far_copy(t).wait()
        re = terms + nn(x, fbuf[t, 0].reshape(B, B))
        acc = re + turn(nn(x, fbuf[t, 1].reshape(B, B)))
        pb = acc.astype(BF)
        ref = (p2, p1, p3, p0)[t // 4]
        ref[t % 4] = acc if ref is p0 else pb
    if coef:
        cpart[row] = coef_of(basis[:, row], pb).astype(BF)


def both_terms(tab, near, far, basis, coefs, pieces, coef):
    anyspec = pl.BlockSpec(memory_space=pl.ANY)
    vmem = pl.BlockSpec(memory_space=pltpu.VMEM)
    outs = [jax.ShapeDtypeStruct(QUARTER, F32)] + [jax.ShapeDtypeStruct(QUARTER, BF)] * 3
    if coef:
        outs.append(jax.ShapeDtypeStruct((NBLK, K, 2 * R), BF))
    sizes = [p.shape[0] for p in pieces]
    return pl.pallas_call(
        functools.partial(both_kernel, sizes, coef),
        out_shape=outs,
        in_specs=[pl.BlockSpec(memory_space=pltpu.SMEM), anyspec, anyspec, vmem]
        + [anyspec] * (1 + len(pieces)),
        out_specs=[vmem] * len(outs),
        scratch_shapes=[
            pltpu.VMEM((32, 2 * R, B), BF),
            pltpu.VMEM((512, K, 2 * R), BF),
            pltpu.VMEM((4, B, 2 * R), BF),
            pltpu.VMEM(QUARTER, F32),
            pltpu.VMEM((NBLK, 2, 4, B, B), BF),
            pltpu.VMEM((NBLK, 2, 8, K, B), BF),
            pltpu.SemaphoreType.DMA((32,)),
            pltpu.SemaphoreType.DMA((1,)),
            pltpu.SemaphoreType.DMA((NBLK,)),
            pltpu.SemaphoreType.DMA((NBLK,)),
        ],
        compiler_params=pltpu.CompilerParams(vmem_limit_bytes=VMEM),
        cost_estimate=pl.CostEstimate(
            flops=10_000_000_000, bytes_accessed=30_000_000, transcendentals=0
        ),
    )(tab, near, far, basis, coefs, *pieces)


def gather_coef(c):
    return lax.all_gather(c, "rows", axis=0, tiled=True)


def gather_vector(v):
    beside = jnp.concatenate([send_row(v[2:], 1), send_row(v[:2], -1)], axis=0)
    mine = [v] + [send_x(v, d) for d in (1, 2, 3)]
    return mine + [beside] + [send_x(beside, d) for d in (1, 2, 3)]


def sum_x(own, parts):
    return (own + parts[1]) + (parts[0] + parts[2])


def all_sum(keep, give):
    m = keep + send_core(give)
    for send in (send_x, send_y, send_z):
        m = sum_x(m, [send(m, d) for d in (1, 2, 3)])
    return m, send_core(m)


HALVES = 5 * R // 4


def gram_kernel(core, f, g, e, keep, give, whole):
    def inner(a, b):
        acc = jnp.zeros((2 * R, 2 * R), F32)
        for q in range(4):
            acc = acc + nt(a[q], b[q], lax.Precision.HIGHEST)
        return acc[:R, :R] + acc[R:, R:]

    whole[:R, :R] = inner(g, f)
    whole[:R, R:] = inner(g, g)
    whole[R : 2 * R, :R] = inner(e, f)
    whole[R : 2 * R, R:] = inner(e, e)
    cross = inner(g, e)
    whole[2 * R :, :R] = cross[: R // 2]
    whole[2 * R :, R:] = cross[R // 2 :]
    k = core[0]
    keep[...] = whole[pl.ds(pl.multiple_of(k * HALVES, 8), HALVES), :]
    give[...] = whole[pl.ds(pl.multiple_of((1 - k) * HALVES, 8), HALVES), :]


def gram(core, f, g, e):
    vmem = pl.BlockSpec(memory_space=pltpu.VMEM)
    return pl.pallas_call(
        gram_kernel,
        in_specs=[pl.BlockSpec(memory_space=pltpu.SMEM), vmem, vmem, vmem],
        out_specs=[vmem, vmem],
        out_shape=[jax.ShapeDtypeStruct((HALVES, 2 * R), F32)] * 2,
        scratch_shapes=[pltpu.VMEM((2 * HALVES, 2 * R), F32)],
        compiler_params=pltpu.CompilerParams(vmem_limit_bytes=VMEM),
    )(core, f, g, e)


def both_halves(m):
    zero = jnp.zeros((R, R), m.dtype)
    return jnp.concatenate(
        [jnp.concatenate([m, zero], axis=1), jnp.concatenate([zero, m], axis=1)], axis=0
    )


def tn(a, b):
    return lax.dot_general(a, b, (((0,), (0,)), ((), ())), preferred_element_type=F32)


def solve(a):
    n = 2 * R
    eye = lax.broadcasted_iota(jnp.int32, (n, n), 0) == lax.broadcasted_iota(jnp.int32, (n, n), 1)
    diag = jnp.where(eye, a[:, :n], 0.0)
    down = lax.rsqrt(jnp.sum(diag, axis=1, keepdims=True))
    across = lax.rsqrt(jnp.sum(diag, axis=0, keepdims=True))
    a = a * down * jnp.concatenate([across, jnp.ones((1, n), F32)], axis=1)
    sub = lax.broadcasted_iota(jnp.int32, (8, 1), 0)
    groups = [a[i : i + 8] for i in range(0, 2 * R, 8)]
    for k in range(0, 2 * R, 2):
        g, j = k // 8, k % 8
        r0, r1 = groups[g][j : j + 1], groups[g][j + 1 : j + 2]
        d00, d01 = r0[:, k : k + 1], r0[:, k + 1 : k + 2]
        d10, d11 = r1[:, k : k + 1], r1[:, k + 1 : k + 2]
        scale = 1.0 / (d00 * d11 - d01 * d10)
        m0 = (r0 * d11 - r1 * d01) * scale
        m1 = (r1 * d00 - r0 * d10) * scale
        groups = [x - x[:, k : k + 1] * m0 - x[:, k + 1 : k + 2] * m1 for x in groups]
        groups[g] = jnp.where(sub == j, m0, jnp.where(sub == j + 1, m1, groups[g]))
    return jnp.concatenate(groups, axis=0)[:, n : n + R] * down


def update_kernel(info, half, other, guess, *refs):
    pieces, out = refs[:12], refs[12]
    whole, gbuf, buf, sem = refs[13:]
    copies = [pltpu.make_async_copy(guess, gbuf, sem.at[12])]
    copies += [pltpu.make_async_copy(p, buf.at[n], sem.at[n]) for n, p in enumerate(pieces)]
    for c in copies:
        c.start()
    core = info[4]
    whole[pl.ds(pl.multiple_of(core * HALVES, 8), HALVES), :] = half[...]
    whole[pl.ds(pl.multiple_of((1 - core) * HALVES, 8), HALVES), :] = other[...]
    cross = jnp.concatenate([whole[2 * R :, :R], whole[2 * R :, R:]], axis=0)
    zero = jnp.zeros((R, R), F32)
    upper = jnp.concatenate([whole[:R, R:], cross, whole[:R, :R], zero], axis=1)
    lower = jnp.concatenate([cross.T, whole[R : 2 * R, R:], whole[R : 2 * R, :R], zero], axis=1)
    y = solve(jnp.concatenate([upper, lower], axis=0))
    mats = []
    for m in (y[:R], y[R:]):
        high = m.astype(BF)
        mats.append((both_halves(high), both_halves((m - high.astype(F32)).astype(BF))))
    for c in copies:
        c.wait()
    for d in range(4):
        for q in range(4):
            at = pl.ds(pl.multiple_of((info[d] + 4 * q) * B, B), B)
            f, low, g = buf[d, q], buf[4 + d, q], buf[8 + d, q]
            acc = gbuf[at, :] + tn(f, mats[0][0]) + tn(f, mats[0][1]) + tn(low, mats[0][0])
            out[at, :] = acc + tn(g, mats[1][0]) + tn(g, mats[1][1])


def update(info, half, other, guess, f, low, g):
    vmem = pl.BlockSpec(memory_space=pltpu.VMEM)
    return pl.pallas_call(
        update_kernel,
        in_specs=[pl.BlockSpec(memory_space=pltpu.SMEM), vmem, vmem]
        + [pl.BlockSpec(memory_space=pl.ANY)] * 13,
        out_specs=vmem,
        out_shape=jax.ShapeDtypeStruct((NBLK * B, 2 * R), F32),
        scratch_shapes=[
            pltpu.VMEM((2 * HALVES, 2 * R), F32),
            pltpu.VMEM((NBLK * B, 2 * R), F32),
            pltpu.VMEM((12,) + QUARTER, BF),
            pltpu.SemaphoreType.DMA((13,)),
        ],
        compiler_params=pltpu.CompilerParams(vmem_limit_bytes=VMEM),
    )(info, half, other, guess, *f, *low, *g)


def summed(p0, p1, p2, p3):
    return sum_x(p0, [send_x(p, d).astype(F32) for d, p in ((1, p1), (2, p2), (3, p3))])


def summed_coef(cpart):
    return sum_x(cpart.astype(F32), [send_x(cpart, d).astype(F32) for d in (1, 2, 3)])


def shards(rhs, guess, near, near_cols, far_u, far_cols, far_count, basis):
    me_r = lax.axis_index("rows")
    me_c = lax.axis_index("cols")
    ints = lambda *v: jnp.array(v, jnp.int32)

    lane = jnp.arange(16, dtype=jnp.int32)
    order = (me_c + ints(2, 1, 3, 0)[lane // 4]) % SIDE + 4 * (lane % 4)
    ncol = (near_cols - (me_r * NBLK - HALF)).reshape(-1)
    fpos = far_cols.reshape(-1)
    used = jnp.clip(far_count - me_c * 8, 0, 8)
    e = (me_c - jnp.arange(4, dtype=jnp.int32)) % SIDE
    head = [order, ncol, fpos, used]
    slots_first = jnp.concatenate([HALF + lane, lane[:8], HALF + 16 + lane[:8]])
    four = (e[:, None] + ints(0, 4, 8, 12)).reshape(-1)
    beside = (e[:, None] + ints(0, 4, 24, 28)).reshape(-1)
    slots_next = jnp.concatenate([HALF + four, beside])
    tab_first = jnp.concatenate(head + [slots_first]).astype(jnp.int32)
    tab_next = jnp.concatenate(head + [slots_next]).astype(jnp.int32)

    whole = gather_coef(guess_coef(guess, basis))
    g_low, g_high, mine, c_diff = prepare(e, rhs, guess, basis)
    pieces = [g_low, g_high, send_row(g_high, 1), send_row(g_low, -1)]
    p2, p1, p3, p0, turned = near_terms(tab_first, near, pieces, True, (0, 1, 2, 3))
    p0, p1, p2, p3, cpart = far_part(tab_first, far_u, basis, whole, [p0, p1, p2, p3])

    c_first = c_diff - summed_coef(cpart)
    whole = gather_coef(c_first.astype(BF))
    first = mine - summed(p0, p1, p2, p3)
    first_b = first.astype(BF)
    first_all = gather_vector(first_b)
    p0, p1, p2, p3, cpart = both_terms(tab_next, turned, far_u, basis, whole, first_all, True)

    c_image = c_first + summed_coef(cpart)
    whole = gather_coef(c_image.astype(BF))
    image = first + summed(p0, p1, p2, p3)
    pieces = gather_vector(image.astype(BF))
    low = (first - lax.reduce_precision(first, 8, 7)).astype(BF)
    low_all = [low] + [send_x(low, d) for d in (1, 2, 3)]
    p0, p1, p2, p3 = both_terms(tab_next, turned, far_u, basis, whole, pieces, False)
    p1, low_all = lax.optimization_barrier((p1, low_all))
    second = image + summed(p0, p1, p2, p3)

    core = me_r % CORES
    half, other = all_sum(*gram(core.reshape(1), first, image, second))
    info = jnp.concatenate([e, core.reshape(1)])
    return update(info, half, other, guess, first_all[:4], low_all, pieces[:4])


def solution(mesh):
    in_specs = (
        P("rows", None),
        P("rows", None),
        P(None, "rows", "cols", None, None),
        P("rows", "cols"),
        P(None, "rows", "cols", None, None),
        P("rows", "cols"),
        P("rows"),
        P(None, "rows", None, None),
    )
    return jax.shard_map(
        shards, mesh=mesh, in_specs=in_specs, out_specs=P("rows", None), check_vma=False
    )
```

```python
import functools

import jax
import jax.numpy as jnp
from jax import lax
from jax.experimental import pallas as pl
from jax.experimental.pallas import tpu as pltpu
from jax.sharding import PartitionSpec as P

B = 256
K = 32
R = 64
HALF = 8
SIDE = 4
CORES = 2
NBLK = 16
BF = jnp.bfloat16
F32 = jnp.float32


def row_id(z, y, k):
    return (z * SIDE + y) * CORES + k


def shift_y(d):
    return [
        (row_id(z, y, k), row_id(z, (y + d) % SIDE, k))
        for z in range(SIDE) for y in range(SIDE) for k in range(CORES)
    ]


def shift_z(d):
    return [
        (row_id(z, y, k), row_id((z + d) % SIDE, y, k))
        for z in range(SIDE) for y in range(SIDE) for k in range(CORES)
    ]


def send_x(a, d):
    return lax.ppermute(a, "cols", [(x, (x + d) % SIDE) for x in range(SIDE)])


def send_y(a, d):
    return lax.ppermute(a, "rows", shift_y(d))


def send_z(a, d):
    return lax.ppermute(a, "rows", shift_z(d))


def send_core(a):
    return lax.ppermute(a, "rows", [(r, r ^ 1) for r in range(SIDE * SIDE * CORES)])


def send_row(a, d):
    n = SIDE * SIDE * CORES
    return lax.ppermute(a, "rows", [(r, (r + d) % n) for r in range(n)])


def nn(a, b, precision=None):
    return lax.dot_general(
        a, b, (((1,), (0,)), ((), ())), preferred_element_type=F32, precision=precision
    )


def nt(a, b, precision=None):
    return lax.dot_general(
        a, b, (((1,), (1,)), ((), ())), preferred_element_type=F32, precision=precision
    )


def turn(x):
    return jnp.concatenate([-x[R:], x[:R]], axis=0)


def turn_lanes(x):
    return jnp.concatenate([-x[:, R:], x[:, :R]], axis=1)


def full_spec(shape):
    return pl.BlockSpec(shape, lambda *_: (0,) * len(shape))


ORDER, NCOL, FPOS, USED, VSLOT = 0, 16, 80, 208, 224
QUARTER = (4, 2 * R, B)
VMEM = 56 * 2 ** 20


def coef_of(basis, vec):
    both = nt(basis.reshape(2 * K, B), vec)
    return both[:K] + turn_lanes(both[K:])


def guess_coef_kernel(guess, basis, out):
    for i in range(NBLK):
        g = guess[pl.ds(i * B, B), :].astype(BF)
        both = nn(basis[:, i].reshape(2 * K, B), g)
        out[i] = (both[:K] + turn_lanes(both[K:])).astype(BF)


def guess_coef(guess, basis):
    return pl.pallas_call(
        guess_coef_kernel,
        out_shape=jax.ShapeDtypeStruct((NBLK, K, 2 * R), BF),
        compiler_params=pltpu.CompilerParams(vmem_limit_bytes=VMEM),
    )(guess, basis)


def prepare_kernel(tab, rhs, guess, basis, low, high, mine, cd):
    for i in range(NBLK):
        g = guess[pl.ds(i * B, B), :]
        (low if i < HALF else high)[i % HALF] = g.astype(BF).T
        d = (rhs[pl.ds(i * B, B), :] - g).astype(BF)
        both = nn(basis[:, i].reshape(2 * K, B), d)
        cd[i] = both[:K] + turn_lanes(both[K:])
    for q in range(4):
        at = pl.ds(pl.multiple_of((tab[0] + 4 * q) * B, B), B)
        mine[q] = (rhs[at, :] - guess[at, :]).T


def prepare(tab, rhs, guess, basis):
    vmem = pl.BlockSpec(memory_space=pltpu.VMEM)
    return pl.pallas_call(
        prepare_kernel,
        in_specs=[pl.BlockSpec(memory_space=pltpu.SMEM), vmem, vmem, vmem],
        out_specs=[vmem] * 4,
        out_shape=[
            jax.ShapeDtypeStruct((HALF, 2 * R, B), BF),
            jax.ShapeDtypeStruct((HALF, 2 * R, B), BF),
            jax.ShapeDtypeStruct(QUARTER, F32),
            jax.ShapeDtypeStruct((NBLK, K, 2 * R), F32),
        ],
        compiler_params=pltpu.CompilerParams(vmem_limit_bytes=VMEM),
    )(tab, rhs, guess, basis)


LOOK = 3


def near_kernel(sizes, first, groups, tab, near, *refs):
    n, m = len(sizes), len(groups)
    pieces, outs = refs[:n], refs[n : n + m]
    turned = refs[n + m] if first else None
    vt, nbuf, vsem, nsem = refs[n + m + first : n + m + 4 + first]
    tbuf, tsem = refs[n + m + 5 :] if first else (None, None)
    steps = range(4 * groups[0], 4 * groups[0] + 4 * m)

    def near_copy(t):
        source = near.at[:, tab[ORDER + t]] if first else near.at[t]
        return pltpu.make_async_copy(source, nbuf.at[t - steps[0]], nsem.at[t - steps[0]])

    def turned_copy(t):
        return pltpu.make_async_copy(tbuf.at[t], turned.at[t], tsem.at[t])

    copies = []
    for piece, size in zip(pieces, sizes):
        for b in range(size):
            i = len(copies)
            copies.append(pltpu.make_async_copy(piece.at[b], vt.at[tab[VSLOT + i]], vsem.at[i]))
    for c in copies:
        c.start()
    for t in steps[:LOOK]:
        near_copy(t).start()
    for c in copies:
        c.wait()
    for t in steps:
        if t + LOOK in steps:
            near_copy(t + LOOK).start()
        near_copy(t).wait()
        row = tab[ORDER + t]
        re = jnp.zeros((2 * R, B), F32)
        im = jnp.zeros((2 * R, B), F32)
        for s in range(4):
            x = vt[tab[NCOL + row * 4 + s]]
            a, b = nbuf[t - steps[0], 0, s], nbuf[t - steps[0], 1, s]
            if first:
                a, b = a.T, b.T
                tbuf[t, 0, s] = a
                tbuf[t, 1, s] = b
            re = re + nn(x, a)
            im = im + nn(x, b)
        if first:
            turned_copy(t).start()
        out = outs[t // 4 - groups[0]]
        out[t % 4] = (re + turn(im)).astype(out.dtype)
    if first:
        for t in steps:
            turned_copy(t).wait()


def near_terms(tab, near, pieces, first, groups):
    anyspec = pl.BlockSpec(memory_space=pl.ANY)
    vmem = pl.BlockSpec(memory_space=pltpu.VMEM)
    sizes = [p.shape[0] for p in pieces]
    count = 4 * len(groups)
    held = (count, 2, 4, B, B)
    scratch = [
        pltpu.VMEM((32, 2 * R, B), BF),
        pltpu.VMEM(held, BF),
        pltpu.SemaphoreType.DMA((32,)),
        pltpu.SemaphoreType.DMA((count,)),
    ]
    if first:
        scratch += [pltpu.VMEM(held, BF), pltpu.SemaphoreType.DMA((count,))]
    outs = [jax.ShapeDtypeStruct(QUARTER, F32 if g == 3 else BF) for g in groups]
    return pl.pallas_call(
        functools.partial(near_kernel, sizes, first, groups),
        out_shape=outs + [jax.ShapeDtypeStruct(held, BF)] * first,
        in_specs=[pl.BlockSpec(memory_space=pltpu.SMEM)] + [anyspec] * (1 + len(pieces)),
        out_specs=[vmem] * len(groups) + [anyspec] * first,
        scratch_shapes=scratch,
        compiler_params=pltpu.CompilerParams(vmem_limit_bytes=VMEM),
        cost_estimate=pl.CostEstimate(
            flops=2_000_000_000 * len(groups),
            bytes_accessed=5_000_000 * len(groups),
            transcendentals=0,
        ),
    )(tab, near, *pieces)


def far_part_kernel(tab, far, basis, coefs, t0, t1, t2, t3, p0, p1, p2, p3, cpart, cs, fx, fbuf, sem, fsem):
    copy = pltpu.make_async_copy(coefs, cs, sem.at[0])
    copy.start()

    def far_copy(t):
        return pltpu.make_async_copy(far.at[:, tab[ORDER + t]], fbuf.at[t], fsem.at[t])

    for t in range(4):
        far_copy(t).start()
    copy.wait()
    for t in range(4, NBLK):
        far_copy(t).start()
    for phase, (terms, ref) in enumerate(((t2, p2), (t1, p1), (t3, p3), (t0, p0))):
        for q in range(4):
            t = phase * 4 + q
            if t:
                cpart[row] = coef_of(basis[:, row], pb).astype(BF)
            row = tab[ORDER + t]
            used = tab[USED + row]
            for s in range(8):
                col = tab[FPOS + row * 8 + s]
                fx[q, pl.ds(s * K, K), :] = jnp.where(
                    s < used, cs[col], jnp.zeros((K, 2 * R), BF)
                )
            x = fx[q].T
            far_copy(t).wait()
            re = terms[q].astype(F32) + nn(x, fbuf[t, 0].reshape(B, B))
            acc = re + turn(nn(x, fbuf[t, 1].reshape(B, B)))
            pb = acc.astype(BF)
            ref[q] = acc if ref is p0 else pb
    cpart[row] = coef_of(basis[:, row], pb).astype(BF)


def far_part(tab, far, basis, coefs, terms):
    anyspec = pl.BlockSpec(memory_space=pl.ANY)
    vmem = pl.BlockSpec(memory_space=pltpu.VMEM)
    smem = pl.BlockSpec(memory_space=pltpu.SMEM)
    outs = [jax.ShapeDtypeStruct(QUARTER, F32)] + [jax.ShapeDtypeStruct(QUARTER, BF)] * 3
    outs.append(jax.ShapeDtypeStruct((NBLK, K, 2 * R), BF))
    return pl.pallas_call(
        far_part_kernel,
        out_shape=outs,
        in_specs=[smem, anyspec, vmem, anyspec] + [vmem] * 4,
        out_specs=[vmem] * len(outs),
        scratch_shapes=[
            pltpu.VMEM((512, K, 2 * R), BF),
            pltpu.VMEM((4, B, 2 * R), BF),
            pltpu.VMEM((NBLK, 2, 8, K, B), BF),
            pltpu.SemaphoreType.DMA((1,)),
            pltpu.SemaphoreType.DMA((NBLK,)),
        ],
        compiler_params=pltpu.CompilerParams(vmem_limit_bytes=VMEM),
        cost_estimate=pl.CostEstimate(
            flops=2_000_000_000, bytes_accessed=13_000_000, transcendentals=0
        ),
    )(tab, far, basis, coefs, *terms)


def both_kernel(sizes, coef, tab, turned, far, basis, coefs, *refs):
    n = len(sizes)
    pieces = refs[:n]
    p0, p1, p2, p3 = refs[n : n + 4]
    cpart = refs[n + 4] if coef else None
    vt, cs, fx, ahead, nbuf, fbuf, vsem, csem, nsem, fsem = refs[n + 4 + coef :]

    def near_copy(t):
        return pltpu.make_async_copy(turned.at[t], nbuf.at[t], nsem.at[t])

    def far_copy(t):
        return pltpu.make_async_copy(far.at[:, tab[ORDER + t]], fbuf.at[t], fsem.at[t])

    copies = []
    for piece, size in zip(pieces, sizes):
        for b in range(size):
            m = len(copies)
            copies.append(pltpu.make_async_copy(piece.at[b], vt.at[tab[VSLOT + m]], vsem.at[m]))
    for c in copies:
        c.start()
    near_copy(0).start()
    near_copy(1).start()
    whole = pltpu.make_async_copy(coefs, cs, csem.at[0])
    for c in copies:
        c.wait()
    whole.start()
    near_copy(2).start()
    near_copy(3).start()
    far_copy(0).start()
    far_copy(1).start()

    def near_part(t):
        near_copy(t).wait()
        row = tab[ORDER + t]
        re = jnp.zeros((2 * R, B), F32)
        im = jnp.zeros((2 * R, B), F32)
        for s in range(4):
            x = vt[tab[NCOL + row * 4 + s]]
            re = re + nn(x, nbuf[t, 0, s])
            im = im + nn(x, nbuf[t, 1, s])
        return re + turn(im)

    for t in range(4):
        ahead[t] = near_part(t)
        near_copy(t + 4).start()
        if t >= 2:
            far_copy(t).start()
    whole.wait()
    for t in range(NBLK):
        if t + 4 < NBLK:
            if t + 8 < NBLK and t < 12:
                near_copy(t + 8).start()
            far_copy(t + 4).start()
        terms = ahead[t] if t < 4 else near_part(t)
        if coef and t:
            cpart[row] = coef_of(basis[:, row], pb).astype(BF)
        row = tab[ORDER + t]
        used = tab[USED + row]
        for s in range(8):
            col = tab[FPOS + row * 8 + s]
            fx[t % 4, pl.ds(s * K, K), :] = jnp.where(
                s < used, cs[col], jnp.zeros((K, 2 * R), BF)
            )
        x = fx[t % 4].T
        far_copy(t).wait()
        re = terms + nn(x, fbuf[t, 0].reshape(B, B))
        acc = re + turn(nn(x, fbuf[t, 1].reshape(B, B)))
        pb = acc.astype(BF)
        ref = (p2, p1, p3, p0)[t // 4]
        ref[t % 4] = acc if ref is p0 else pb
    if coef:
        cpart[row] = coef_of(basis[:, row], pb).astype(BF)


def both_terms(tab, near, far, basis, coefs, pieces, coef):
    anyspec = pl.BlockSpec(memory_space=pl.ANY)
    vmem = pl.BlockSpec(memory_space=pltpu.VMEM)
    outs = [jax.ShapeDtypeStruct(QUARTER, F32)] + [jax.ShapeDtypeStruct(QUARTER, BF)] * 3
    if coef:
        outs.append(jax.ShapeDtypeStruct((NBLK, K, 2 * R), BF))
    sizes = [p.shape[0] for p in pieces]
    return pl.pallas_call(
        functools.partial(both_kernel, sizes, coef),
        out_shape=outs,
        in_specs=[pl.BlockSpec(memory_space=pltpu.SMEM), anyspec, anyspec, vmem]
        + [anyspec] * (1 + len(pieces)),
        out_specs=[vmem] * len(outs),
        scratch_shapes=[
            pltpu.VMEM((32, 2 * R, B), BF),
            pltpu.VMEM((512, K, 2 * R), BF),
            pltpu.VMEM((4, B, 2 * R), BF),
            pltpu.VMEM(QUARTER, F32),
            pltpu.VMEM((NBLK, 2, 4, B, B), BF),
            pltpu.VMEM((NBLK, 2, 8, K, B), BF),
            pltpu.SemaphoreType.DMA((32,)),
            pltpu.SemaphoreType.DMA((1,)),
            pltpu.SemaphoreType.DMA((NBLK,)),
            pltpu.SemaphoreType.DMA((NBLK,)),
        ],
        compiler_params=pltpu.CompilerParams(vmem_limit_bytes=VMEM),
        cost_estimate=pl.CostEstimate(
            flops=10_000_000_000, bytes_accessed=30_000_000, transcendentals=0
        ),
    )(tab, near, far, basis, coefs, *pieces)


def gather_coef(c):
    return lax.all_gather(c, "rows", axis=0, tiled=True)


def gather_vector(v):
    beside = jnp.concatenate([send_row(v[2:], 1), send_row(v[:2], -1)], axis=0)
    mine = [v] + [send_x(v, d) for d in (1, 2, 3)]
    return mine + [beside] + [send_x(beside, d) for d in (1, 2, 3)]


def sum_x(own, parts):
    return (own + parts[1]) + (parts[0] + parts[2])


def all_sum(keep, give):
    m = keep + send_core(give)
    for send in (send_x, send_y, send_z):
        m = sum_x(m, [send(m, d) for d in (1, 2, 3)])
    return m, send_core(m)


HALVES = 5 * R // 4


def gram_kernel(core, f, g, e, keep, give, whole):
    def inner(a, b):
        acc = jnp.zeros((2 * R, 2 * R), F32)
        for q in range(4):
            acc = acc + nt(a[q], b[q], lax.Precision.HIGHEST)
        return acc[:R, :R] + acc[R:, R:]

    whole[:R, :R] = inner(g, f)
    whole[:R, R:] = inner(g, g)
    whole[R : 2 * R, :R] = inner(e, f)
    whole[R : 2 * R, R:] = inner(e, e)
    cross = inner(g, e)
    whole[2 * R :, :R] = cross[: R // 2]
    whole[2 * R :, R:] = cross[R // 2 :]
    k = core[0]
    keep[...] = whole[pl.ds(pl.multiple_of(k * HALVES, 8), HALVES), :]
    give[...] = whole[pl.ds(pl.multiple_of((1 - k) * HALVES, 8), HALVES), :]


def gram(core, f, g, e):
    vmem = pl.BlockSpec(memory_space=pltpu.VMEM)
    return pl.pallas_call(
        gram_kernel,
        in_specs=[pl.BlockSpec(memory_space=pltpu.SMEM), vmem, vmem, vmem],
        out_specs=[vmem, vmem],
        out_shape=[jax.ShapeDtypeStruct((HALVES, 2 * R), F32)] * 2,
        scratch_shapes=[pltpu.VMEM((2 * HALVES, 2 * R), F32)],
        compiler_params=pltpu.CompilerParams(vmem_limit_bytes=VMEM),
    )(core, f, g, e)


def both_halves(m):
    zero = jnp.zeros((R, R), m.dtype)
    return jnp.concatenate(
        [jnp.concatenate([m, zero], axis=1), jnp.concatenate([zero, m], axis=1)], axis=0
    )


def tn(a, b):
    return lax.dot_general(a, b, (((0,), (0,)), ((), ())), preferred_element_type=F32)


def solve(a):
    n = 2 * R
    eye = lax.broadcasted_iota(jnp.int32, (n, n), 0) == lax.broadcasted_iota(jnp.int32, (n, n), 1)
    diag = jnp.where(eye, a[:, :n], 0.0)
    down = lax.rsqrt(jnp.sum(diag, axis=1, keepdims=True))
    across = lax.rsqrt(jnp.sum(diag, axis=0, keepdims=True))
    a = a * down * jnp.concatenate([across, jnp.ones((1, n), F32)], axis=1)
    sub = lax.broadcasted_iota(jnp.int32, (8, 1), 0)
    groups = [a[i : i + 8] for i in range(0, 2 * R, 8)]
    for k in range(0, 2 * R, 2):
        g, j = k // 8, k % 8
        r0, r1 = groups[g][j : j + 1], groups[g][j + 1 : j + 2]
        d00, d01 = r0[:, k : k + 1], r0[:, k + 1 : k + 2]
        d10, d11 = r1[:, k : k + 1], r1[:, k + 1 : k + 2]
        scale = 1.0 / (d00 * d11 - d01 * d10)
        m0 = (r0 * d11 - r1 * d01) * scale
        m1 = (r1 * d00 - r0 * d10) * scale
        groups = [x - x[:, k : k + 1] * m0 - x[:, k + 1 : k + 2] * m1 for x in groups]
        groups[g] = jnp.where(sub == j, m0, jnp.where(sub == j + 1, m1, groups[g]))
    return jnp.concatenate(groups, axis=0)[:, n : n + R] * down


def update_kernel(info, half, other, guess, *refs):
    pieces, out = refs[:12], refs[12]
    whole, gbuf, buf, sem = refs[13:]
    copies = [pltpu.make_async_copy(guess, gbuf, sem.at[12])]
    copies += [pltpu.make_async_copy(p, buf.at[n], sem.at[n]) for n, p in enumerate(pieces)]
    for c in copies:
        c.start()
    core = info[4]
    whole[pl.ds(pl.multiple_of(core * HALVES, 8), HALVES), :] = half[...]
    whole[pl.ds(pl.multiple_of((1 - core) * HALVES, 8), HALVES), :] = other[...]
    cross = jnp.concatenate([whole[2 * R :, :R], whole[2 * R :, R:]], axis=0)
    zero = jnp.zeros((R, R), F32)
    upper = jnp.concatenate([whole[:R, R:], cross, whole[:R, :R], zero], axis=1)
    lower = jnp.concatenate([cross.T, whole[R : 2 * R, R:], whole[R : 2 * R, :R], zero], axis=1)
    y = solve(jnp.concatenate([upper, lower], axis=0))
    mats = []
    for m in (y[:R], y[R:]):
        high = m.astype(BF)
        mats.append((both_halves(high), both_halves((m - high.astype(F32)).astype(BF))))
    for c in copies:
        c.wait()
    for d in range(4):
        for q in range(4):
            at = pl.ds(pl.multiple_of((info[d] + 4 * q) * B, B), B)
            f, low, g = buf[d, q], buf[4 + d, q], buf[8 + d, q]
            acc = gbuf[at, :] + tn(f, mats[0][0]) + tn(f, mats[0][1]) + tn(low, mats[0][0])
            out[at, :] = acc + tn(g, mats[1][0]) + tn(g, mats[1][1])


def update(info, half, other, guess, f, low, g):
    vmem = pl.BlockSpec(memory_space=pltpu.VMEM)
    return pl.pallas_call(
        update_kernel,
        in_specs=[pl.BlockSpec(memory_space=pltpu.SMEM), vmem, vmem]
        + [pl.BlockSpec(memory_space=pl.ANY)] * 13,
        out_specs=vmem,
        out_shape=jax.ShapeDtypeStruct((NBLK * B, 2 * R), F32),
        scratch_shapes=[
            pltpu.VMEM((2 * HALVES, 2 * R), F32),
            pltpu.VMEM((NBLK * B, 2 * R), F32),
            pltpu.VMEM((12,) + QUARTER, BF),
            pltpu.SemaphoreType.DMA((13,)),
        ],
        compiler_params=pltpu.CompilerParams(vmem_limit_bytes=VMEM),
    )(info, half, other, guess, *f, *low, *g)


def summed(p0, p1, p2, p3):
    return sum_x(p0, [send_x(p, d).astype(F32) for d, p in ((1, p1), (2, p2), (3, p3))])


def summed_coef(cpart):
    return sum_x(cpart.astype(F32), [send_x(cpart, d).astype(F32) for d in (1, 2, 3)])


def shards(rhs, guess, near, near_cols, far_u, far_cols, far_count, basis):
    me_r = lax.axis_index("rows")
    me_c = lax.axis_index("cols")
    ints = lambda *v: jnp.array(v, jnp.int32)

    lane = jnp.arange(16, dtype=jnp.int32)
    order = (me_c + ints(2, 1, 3, 0)[lane // 4]) % SIDE + 4 * (lane % 4)
    ncol = (near_cols - (me_r * NBLK - HALF)).reshape(-1)
    fpos = far_cols.reshape(-1)
    used = jnp.clip(far_count - me_c * 8, 0, 8)
    e = (me_c - jnp.arange(4, dtype=jnp.int32)) % SIDE
    head = [order, ncol, fpos, used]
    slots_first = jnp.concatenate([HALF + lane, lane[:8], HALF + 16 + lane[:8]])
    four = (e[:, None] + ints(0, 4, 8, 12)).reshape(-1)
    beside = (e[:, None] + ints(0, 4, 24, 28)).reshape(-1)
    slots_next = jnp.concatenate([HALF + four, beside])
    tab_first = jnp.concatenate(head + [slots_first]).astype(jnp.int32)
    tab_next = jnp.concatenate(head + [slots_next]).astype(jnp.int32)

    whole = gather_coef(guess_coef(guess, basis))
    g_low, g_high, mine, c_diff = prepare(e, rhs, guess, basis)
    pieces = [g_low, g_high, send_row(g_high, 1), send_row(g_low, -1)]
    p2, p1, p3, p0, turned = near_terms(tab_first, near, pieces, True, (0, 1, 2, 3))
    p0, p1, p2, p3, cpart = far_part(tab_first, far_u, basis, whole, [p0, p1, p2, p3])

    c_first = c_diff - summed_coef(cpart)
    whole = gather_coef(c_first.astype(BF))
    first = mine - summed(p0, p1, p2, p3)
    first_b = first.astype(BF)
    first_all = gather_vector(first_b)
    p0, p1, p2, p3, cpart = both_terms(tab_next, turned, far_u, basis, whole, first_all, True)

    c_image = c_first + summed_coef(cpart)
    whole = gather_coef(c_image.astype(BF))
    image = first + summed(p0, p1, p2, p3)
    pieces = gather_vector(image.astype(BF))
    low = (first - lax.reduce_precision(first, 8, 7)).astype(BF)
    low_all = [low] + [send_x(low, d) for d in (1, 2, 3)]
    p0, p1, p2, p3 = both_terms(tab_next, turned, far_u, basis, whole, pieces, False)
    p1, low_all = lax.optimization_barrier((p1, low_all))
    second = image + summed(p0, p1, p2, p3)

    core = me_r % CORES
    half, other = all_sum(*gram(core.reshape(1), first, image, second))
    info = jnp.concatenate([e, core.reshape(1)])
    return update(info, half, other, guess, first_all[:4], low_all, pieces[:4])


def solution(mesh):
    in_specs = (
        P("rows", None),
        P("rows", None),
        P(None, "rows", "cols", None, None),
        P("rows", "cols"),
        P(None, "rows", "cols", None, None),
        P("rows", "cols"),
        P("rows"),
        P(None, "rows", None, None),
    )
    return jax.shard_map(
        shards, mesh=mesh, in_specs=in_specs, out_specs=P("rows", None), check_vma=False
    )
```
